32 devices in a mesh: groups: 1, seq: 32 (over z, y, x, core).
Axes of the slice: x: 2, y: 2, z: 4, core: 2. Of those that a mesh axis runs over, the one named last changes fastest.
Arguments:
- q_gate: bfloat16 [4096, 4096], P(('groups', 'seq')), may hold values from -6 to 6
- values_in: bfloat16 [4096, 4096], P(('groups', 'seq')), may hold values from -6 to 6
- decay_rate: float32 [4096, 16], replicated, as said below
- residue: float32 [4096, 16], replicated, may hold values from -3 to 3
- skip_gain: float32 [4096], replicated, may hold values from 0.5 to 1.5
- out_weight: bfloat16 [4096, 2048], P('seq'), may hold values from -0.09375 to 0.09375
Outputs:
- mixed: bfloat16 [4096, 2048], P(('groups', 'seq'))
The draws below stay inside these ranges and needn't reach their ends.
Inputs may be any that keep to these rules, and one draw needn't show every extreme that they name: `decay_rate`: every rate is positive and at most about 1/30.
All inputs are finite; a program needn't handle non-finite values.
Results may differ from the reference program's by a relative error of at most 0.0052.
Values may be sent and summed in bfloat16 or wider, within the bound.
No kernel may reach another device: no remote copies, remote signals or barrier semaphores. Data moves between devices by JAX's collectives and lax.ppermute only.
A program may use at most 256 MiB of HBM per device.

```python
import math
import jax
import jax.numpy as jnp
from jax import lax

D = 4096
D_OUT = 2048
ORDER = 16
BLOCK = 32
TOKENS = 4096


def draw_decay_rate(key, part):
    first, second, third = jax.random.split(jax.random.fold_in(key, 11), 3)
    slow = jnp.exp(jax.random.uniform(first, (D, ORDER), jnp.float32, math.log(0.05 / TOKENS), math.log(2.0 / TOKENS)))
    fast = jnp.exp(jax.random.uniform(second, (D, ORDER), jnp.float32, math.log(1.0 / 50.0), math.log(1.0 / 30.0)))
    share_slow = 0.5
    picked = jax.random.uniform(third, (D, ORDER), jnp.float32) < share_slow
    return jnp.where(picked, slow, fast).astype(jnp.float32)


def block_scale(own_key, extent, cuts, smallest, high):
    level = 1.0
    for axis_at, blocks in cuts:
        draws = jax.random.uniform(jax.random.fold_in(jax.random.fold_in(own_key, 6), axis_at), (blocks,), jnp.float32, smallest / len(cuts), high / len(cuts))
        level = level * jnp.repeat(jnp.exp(draws), extent[axis_at] // blocks).reshape((-1,) + (1,) * (len(extent) - 1 - axis_at))
    return level


def normal_values(rng, shape, scale, bound, cuts=(), held_as=jnp.bfloat16):
    gain = block_scale(rng, shape, cuts, -0.22, 0.18) if cuts else 1.0
    result = jax.random.normal(rng, shape, jnp.float32) * scale * gain
    return jnp.minimum(jnp.maximum(result, -bound), bound).astype(held_as)


def setup_inputs(seed: int = 0, part: int = 0) -> dict:
    streams_of = jax.random.split(jax.random.key(seed), 7)
    part_splits = jax.random.split(jax.random.fold_in(streams_of[6], part), 7)
    return {
        "q_gate": normal_values(part_splits[0], (TOKENS, D), 1.0, 6.0, ((0, 32),)),
        "values_in": normal_values(part_splits[1], (TOKENS, D), 1.0, 6.0, ((0, 32),)),
        "decay_rate": draw_decay_rate(jax.random.fold_in(streams_of[6], 71), part),
        "residue": normal_values(streams_of[3], (D, ORDER), 0.5, 3.0, (), jnp.float32),
        "skip_gain": jnp.clip(jax.random.uniform(streams_of[4], (D,), jnp.float32, 0.5, 1.5), 0.5, 1.5),
        "out_weight": normal_values(streams_of[5], (D, D_OUT), D ** -0.5, 0.09375, ((0, 32),)),
    }


def gated_group(q_part, value_part, rate_part, residue_part, skip_part):
    width = q_part.shape[1]
    block_count = TOKENS // BLOCK
    rate_modes = rate_part.T
    mode_scale = jnp.sqrt(-jnp.expm1(-2.0 * rate_modes))
    mode_coef = residue_part.T * mode_scale
    position = jnp.arange(BLOCK, dtype=jnp.float32)
    tap_values = lax.optimization_barrier(jnp.sum(mode_coef[None] * jnp.exp(-position[:, None, None] * rate_modes[None]), axis=1))
    tap_round = tap_values.astype(jnp.bfloat16)
    offsets = jnp.arange(BLOCK)[:, None] - jnp.arange(BLOCK)[None, :]
    toeplitz = jnp.where((offsets >= 0)[:, :, None], tap_round[jnp.maximum(offsets, 0)], jnp.zeros((), jnp.bfloat16))
    blocked = value_part.reshape(block_count, BLOCK, width).astype(jnp.float32)
    local_part = jnp.einsum('tsg,nsg->ntg', toeplitz.astype(jnp.float32), blocked, precision=lax.Precision.HIGHEST)
    end_weight = jnp.exp(-(BLOCK - 1 - position)[:, None, None] * rate_modes[None])
    block_ends = jnp.einsum('tkg,ntg->nkg', end_weight, blocked, precision=lax.Precision.HIGHEST)
    step_decay = jnp.exp(-BLOCK * rate_modes)

    def advance(carry_state, inflow):
        return (step_decay * carry_state + inflow, carry_state)
    _, starts = lax.scan(advance, jnp.zeros((ORDER, width), jnp.float32), block_ends)
    reach_table = mode_coef[None] * jnp.exp(-(position + 1.0)[:, None, None] * rate_modes[None])
    correction = jnp.einsum('tkg,nkg->ntg', reach_table, starts, precision=lax.Precision.HIGHEST)
    conv = (local_part + correction).reshape(TOKENS, width)
    gated = q_part.astype(jnp.float32) * (conv + skip_part[None] * value_part.astype(jnp.float32))
    return gated.astype(jnp.bfloat16)

def reference(q_gate, values_in, decay_rate, residue, skip_gain, out_weight):
    group_width = min(512, D)
    group_count = D // group_width
    q_groups = q_gate.reshape(TOKENS, group_count, group_width).transpose(1, 0, 2)
    value_groups = values_in.reshape(TOKENS, group_count, group_width).transpose(1, 0, 2)
    rate_groups = decay_rate.reshape(group_count, group_width, ORDER)
    residue_groups = residue.reshape(group_count, group_width, ORDER)
    skip_groups = skip_gain.reshape(group_count, group_width)

    def one_group(inputs):
        return gated_group(inputs[0], inputs[1], inputs[2], inputs[3], inputs[4])
    gated_all = lax.map(one_group, (q_groups, value_groups, rate_groups, residue_groups, skip_groups))
    gated = gated_all.transpose(1, 0, 2).reshape(TOKENS, D)
    return jnp.dot(gated, out_weight, preferred_element_type=jnp.float32).astype(jnp.bfloat16)
```

```python
import functools

import jax
import jax.numpy as jnp
from jax import lax
from jax.experimental import pallas as pl
from jax.experimental.pallas import tpu as pltpu
from jax.sharding import PartitionSpec as P

BLOCK = 32
LANES = 128
TEAM = 4
WEIGHT_PARTS = 4
VMEM_LIMIT = 32 * 1024 * 1024

f32 = jnp.float32
bf16 = jnp.bfloat16


def vmem(count):
    return [pl.BlockSpec(memory_space=pltpu.VMEM)] * count


def smem():
    return pl.BlockSpec(memory_space=pltpu.SMEM)


def call(kernel, out_shape, scratch=(), flops=0, moved=0):
    outs = jax.tree.leaves(out_shape)

    def run(info, *args):
        return pl.pallas_call(
            kernel,
            out_shape=out_shape,
            in_specs=[smem()] + vmem(len(args)),
            out_specs=jax.tree.map(lambda _: pl.BlockSpec(memory_space=pltpu.VMEM), out_shape),
            scratch_shapes=list(scratch),
            compiler_params=pltpu.CompilerParams(vmem_limit_bytes=VMEM_LIMIT),
            cost_estimate=pl.CostEstimate(flops=flops, bytes_accessed=moved, transcendentals=0),
        )(info, *args)

    return run


def split_kernel(team, depth, info_ref, *refs):
    me = info_ref[0]
    sources, outs = refs[: len(refs) // (team + 1)], refs[len(refs) // (team + 1) :]
    runs = sources[0].shape[1] // (team * depth)
    for which, source in enumerate(sources):
        for step in range(team):
            out = outs[which * team + step]
            for run in range(runs):
                at = pl.multiple_of((run * team + (me ^ step)) * depth, depth)
                out[:, run * depth : (run + 1) * depth] = source[:, pl.ds(at, depth)]


def split_channels(info, team, depth, sources):
    rows, width = sources[0].shape
    if depth % LANES == 0:
        share = jax.ShapeDtypeStruct((rows, width // team), sources[0].dtype)
        pieces = call(
            functools.partial(split_kernel, team, depth),
            [share] * (team * len(sources)),
            moved=2 * len(sources) * sources[0].size * sources[0].dtype.itemsize,
        )(info, *sources)
        return [pieces[n * team : (n + 1) * team] for n in range(len(sources))]
    out = []
    for source in sources:
        cut = source.reshape(rows, width // (team * depth), team, depth)
        out.append(
            [
                lax.dynamic_index_in_dim(cut, info[0] ^ step, 2, keepdims=False).reshape(rows, -1)
                for step in range(team)
            ]
        )
    return out


def reach_tables(rate, coef, reach, decay8):
    order = rate.shape[0]
    step = lax.broadcasted_iota(jnp.int32, (8, LANES), 0).astype(f32) + 1.0
    for k in range(order):
        reach[k] = coef[k : k + 1] * jnp.exp(-step * rate[k : k + 1])
        decay8[k] = jnp.exp(jnp.broadcast_to(-8.0 * rate[k : k + 1], (8, LANES)))


def local_kernel(info_ref, *refs):
    values = refs[:TEAM]
    rate_ref, coef_ref, skip_ref, y_ref, end_ref, wide, taps, reach, decay8, start = refs[TEAM:]
    me = info_ref[0]
    order = rate_ref.shape[0]
    rows = values[0].shape[0]
    per = rows // BLOCK
    wide[:, :BLOCK, :] = jnp.zeros((wide.shape[0], BLOCK, LANES), f32)

    @pl.loop(0, rate_ref.shape[1] // LANES)
    def _(tile):
        lanes = pl.ds(pl.multiple_of(tile * LANES, LANES), LANES)
        for step in range(TEAM):
            for b in range(per):
                wide[(me ^ step) * per + b, BLOCK:, :] = values[step][
                    b * BLOCK : (b + 1) * BLOCK, lanes
                ].astype(f32)
        rate, coef, skip = rate_ref[:, lanes], coef_ref[:, lanes], skip_ref[:, lanes]
        lam = jnp.exp(-rate)
        power = coef
        for t in range(BLOCK):
            tap = jnp.sum(power, axis=0, keepdims=True).astype(bf16).astype(f32)
            taps[t] = jnp.broadcast_to(tap, (8, LANES))
            power = power * lam
        reach_tables(rate, coef, reach, decay8)
        lam8 = jnp.exp(-8.0 * rate)

        def block(b, state):
            start[...] = state
            y = [skip * wide[b, BLOCK + 8 * i : BLOCK + 8 * i + 8, :] for i in range(BLOCK // 8)]
            for t in range(BLOCK):
                tap = taps[t]
                for i in range(t // 8, BLOCK // 8):
                    at = BLOCK + 8 * i - t
                    y[i] = y[i] + tap * wide[b, at : at + 8, :]
            for k in range(order):
                term = reach[k] * start[k : k + 1, :]
                decay = decay8[k]
                for i in range(BLOCK // 8):
                    y[i] = y[i] + term
                    if i + 1 < BLOCK // 8:
                        term = term * decay
            for i in range(BLOCK // 8):
                y_ref[tile, pl.ds(pl.multiple_of(b * BLOCK + 8 * i, 8), 8), :] = y[i]
            for i in range(BLOCK // 8):
                at = BLOCK + 8 * i
                inflow = jnp.broadcast_to(wide[b, at : at + 1, :], (order, LANES))
                for t in range(1, 8):
                    inflow = lam * inflow + wide[b, at + t : at + t + 1, :]
                state = lam8 * state + inflow
            return state

        end_ref[:, lanes] = lax.fori_loop(0, TEAM * per, block, jnp.zeros((order, LANES), f32))


def gate_kernel(gaps, info_ref, *refs):
    gates = refs[:TEAM]
    y_ref, rate_ref, coef_ref, near_ref = refs[TEAM : TEAM + 4]
    far = refs[TEAM + 4 : TEAM + 4 + gaps]
    out_ref, reach, decay8, start = refs[TEAM + 4 + gaps :]
    me, high = info_ref[0], info_ref[1]
    order = rate_ref.shape[0]
    rows = gates[0].shape[0]
    span = float(TEAM * rows)

    @pl.loop(0, rate_ref.shape[1] // LANES)
    def _(tile):
        lanes = pl.ds(pl.multiple_of(tile * LANES, LANES), LANES)
        rate, coef = rate_ref[:, lanes], coef_ref[:, lanes]
        reach_tables(rate, coef, reach, decay8)
        state = jnp.zeros((order, LANES), f32)
        for gap in range(gaps):
            state = state + jnp.exp(-2.0 * span * gap * rate) * far[gap][:, lanes]
        after = jnp.exp(-span * rate) * state + near_ref[:, lanes]
        state = jnp.where(high == 1, after, state)
        for step in range(TEAM):
            place = me ^ step
            start[...] = state * jnp.exp(-(rows * place).astype(f32) * rate)
            terms = [reach[k] * start[k : k + 1, :] for k in range(order)]
            goes = place ^ (me & 2)
            for at in range(0, rows, 16):
                halves = []
                for half in range(2):
                    total = list(terms)
                    while len(total) > 1:
                        total = [a + b for a, b in zip(total[::2], total[1::2])]
                    here = pl.multiple_of(place * rows + at + 8 * half, 8)
                    halves.append(total[0] + y_ref[tile, pl.ds(here, 8), :])
                    terms = [term * decay8[k] for k, term in enumerate(terms)]
                conv = jnp.concatenate(halves, axis=0)
                gated = gates[step][at : at + 16, lanes].astype(f32) * conv
                out_ref[tile, pl.ds(pl.multiple_of(goes * rows + at, 16), 16), :] = gated.astype(bf16)


def project_kernel(slots, info_ref, own_ref, other_ref, *refs):
    weights, outs, total = refs[:slots], refs[slots : slots + TEAM], refs[-1]
    core = info_ref[2]
    rows = outs[0].shape[0]
    for slot in range(slots):
        group = info_ref[3 + slot]
        left = jnp.concatenate([own_ref[group], other_ref[group]], axis=1)
        product = jnp.dot(left, weights[slot][...], preferred_element_type=f32)
        if slot == 0:
            total[...] = product
        else:
            total[...] += product
    for step, out in enumerate(outs):
        at = (step // 2) * 2 * rows + (core ^ (step & 1)) * rows
        out[...] = total[pl.ds(pl.multiple_of(at, rows), rows), :].astype(out.dtype)


def finish_kernel(parts, info_ref, *refs):
    core = info_ref[2]
    out_ref = refs[-1]
    half = out_ref.shape[1] // 2
    at = 0
    for part in range(parts):
        mine, his, mine_far, his_far = refs[4 * part : 4 * part + 4]
        wide = mine.shape[1]
        near = pl.ds(pl.multiple_of(core * half + at, LANES), wide)
        away = pl.ds(pl.multiple_of((1 - core) * half + at, LANES), wide)
        out_ref[:, near] = (mine[...] + mine_far[...].astype(f32)).astype(bf16)
        out_ref[:, away] = (his[...].astype(f32) + his_far[...].astype(f32)).astype(bf16)
        at += wide


def on_device(q_gate, values_in, decay_rate, residue, skip_gain, out_weight):
    rows, width = q_gate.shape
    depth, features = out_weight.shape
    order = decay_rate.shape[1]
    count = lax.axis_size("seq")
    heights = count // (2 * TEAM)
    mine = lax.axis_index("seq")
    me, core = mine % TEAM, mine % 2
    y, z = (mine // TEAM) % 2, mine // (2 * TEAM)
    share = width // TEAM
    half = features // 2

    def swap(value, bit):
        return lax.ppermute(value, "seq", [(i, i ^ bit) for i in range(count)])

    def up(value, gap, wrap):
        hop = gap * 2 * TEAM
        pairs = [(i, (i + hop) % count) for i in range(count) if wrap or i + hop < count]
        return lax.ppermute(value, "seq", pairs)

    groups = []
    for gap in range(heights):
        at = (z - gap) % heights
        groups += [at * 2 + y, at * 2 + (1 - y)]
    info = jnp.stack([me, y, core] + groups).astype(jnp.int32)

    keep = lax.dynamic_slice_in_dim(out_weight, core * half, half, 1)
    give = lax.dynamic_slice_in_dim(out_weight, (1 - core) * half, half, 1)
    got = swap(give, 1)
    wide = half // WEIGHT_PARTS
    weights = []
    for part in range(WEIGHT_PARTS):
        cut = slice(part * wide, (part + 1) * wide)
        held = jnp.concatenate([keep[:, cut], got[:, cut]], axis=0)
        slots = [held, swap(held, TEAM)]
        for _ in range(1, heights):
            held = up(held, 1, True)
            slots += [held, swap(held, TEAM)]
        weights.append(slots)

    (values,) = split_channels(info, TEAM, depth, [values_in])
    values = [values[0]] + [swap(values[step], step) for step in range(1, TEAM)]
    (gates,) = split_channels(info, TEAM, depth, [q_gate])
    gates = [gates[0]] + [swap(gates[step], step) for step in range(1, TEAM)]
    (rates,), (residues,) = (
        [split[0]] for split in split_channels(info, TEAM, depth, [decay_rate.T, residue.T])
    )
    coef = residues * jnp.sqrt(-jnp.expm1(-2.0 * rates))
    (skips,) = split_channels(info, TEAM, depth, [skip_gain[None]])
    skip = skips[0]

    tiles = share // LANES
    elements = TEAM * rows * share
    blocks = TEAM * rows // BLOCK
    y_local, end = call(
        local_kernel,
        [
            jax.ShapeDtypeStruct((tiles, TEAM * rows, LANES), f32),
            jax.ShapeDtypeStruct((order, share), f32),
        ],
        [
            pltpu.VMEM((blocks, 2 * BLOCK, LANES), f32),
            pltpu.VMEM((BLOCK, 8, LANES), f32),
            pltpu.VMEM((order, 8, LANES), f32),
            pltpu.VMEM((order, 8, LANES), f32),
            pltpu.VMEM((order, LANES), f32),
        ],
        flops=110 * elements,
        moved=6 * elements,
    )(info, *values, rates, coef, skip)

    near = swap(end, TEAM)
    first, second = jnp.where(y == 0, end, near), jnp.where(y == 0, near, end)
    pair_end = jnp.exp(-float(TEAM * rows) * rates) * first + second
    far = [up(pair_end, gap, False) for gap in range(1, heights)]
    gated = call(
        functools.partial(gate_kernel, heights - 1),
        jax.ShapeDtypeStruct((tiles, TEAM * rows, LANES), bf16),
        [
            pltpu.VMEM((order, 8, LANES), f32),
            pltpu.VMEM((order, 8, LANES), f32),
            pltpu.VMEM((order, LANES), f32),
        ],
        flops=40 * elements,
        moved=8 * elements,
    )(info, *gates, y_local, rates, coef, near, *far)
    other = swap(gated, 1)

    if depth % LANES:
        runs = width // (TEAM * depth)

        def by_group(value):
            value = value.transpose(1, 0, 2).reshape(TEAM * rows, runs, depth)
            return value.transpose(1, 0, 2)

        gated, other = by_group(gated), by_group(other)

    finished = []
    for slots in weights:
        shape = functools.partial(jax.ShapeDtypeStruct, (rows, wide))
        sums = call(
            functools.partial(project_kernel, 2 * heights),
            [shape(f32), shape(f32), shape(bf16), shape(bf16)],
            [pltpu.VMEM((TEAM * rows, wide), f32)],
            flops=TEAM * rows * width * wide,
            moved=TEAM * rows * width + width * wide,
        )(info, gated, other, *slots)
        finished += [sums[0]] + [swap(sums[step], step) for step in range(1, TEAM)]
    return call(
        functools.partial(finish_kernel, WEIGHT_PARTS),
        jax.ShapeDtypeStruct((rows, features), bf16),
        moved=rows * features * 8,
    )(info, *finished)


def solution(mesh):
    in_specs = (
        P(("groups", "seq"), None),
        P(("groups", "seq"), None),
        P(),
        P(),
        P(),
        P("seq", None),
    )
    out_specs = P(("groups", "seq"), None)
    return jax.shard_map(
        on_device, mesh=mesh, in_specs=in_specs, out_specs=out_specs, check_vma=False
    )
```

```python
import functools

import jax
import jax.numpy as jnp
from jax import lax
from jax.experimental import pallas as pl
from jax.experimental.pallas import tpu as pltpu
from jax.sharding import PartitionSpec as P

BLOCK = 32
LANES = 128
TEAM = 4
FIRST = 5
VMEM_LIMIT = 32 * 1024 * 1024

f32 = jnp.float32
bf16 = jnp.bfloat16


def call(kernel, out_shape, scratch=(), after=()):
    def body(*refs):
        return kernel(*refs[len(after) :])

    def run(info, *args):
        return pl.pallas_call(
            body,
            out_shape=out_shape,
            in_specs=[pl.BlockSpec(memory_space=pl.ANY)] * len(after)
            + [pl.BlockSpec(memory_space=pltpu.SMEM)]
            + [pl.BlockSpec()] * len(args),
            scratch_shapes=list(scratch),
            compiler_params=pltpu.CompilerParams(vmem_limit_bytes=VMEM_LIMIT),
            cost_estimate=pl.CostEstimate(flops=0, bytes_accessed=0, transcendentals=0),
        )(*after, info, *args)

    return run


def split_kernel(team, depth, plan, info_ref, *refs):
    me = info_ref[0]
    sources, outs = refs[: len(plan)], list(refs[len(plan) :])
    for source, (steps, parts) in zip(sources, plan):
        runs = source.shape[1] // (team * depth)
        for step in range(steps):
            for part in range(parts):
                out = outs.pop(0)
                for run in range(runs // parts):
                    whole = part * (runs // parts) + run
                    at = pl.multiple_of((whole * team + (me ^ step)) * depth, depth)
                    out[:, run * depth : (run + 1) * depth] = source[:, pl.ds(at, depth)]


def split_channels(info, team, depth, sources, plan):
    if depth % LANES == 0:
        shapes = [
            jax.ShapeDtypeStruct((source.shape[0], source.shape[1] // (team * parts)), source.dtype)
            for source, (steps, parts) in zip(sources, plan)
            for _ in range(steps * parts)
        ]
        kernel = functools.partial(split_kernel, team, depth, plan)
        pieces = list(call(kernel, shapes)(info, *sources))
    else:
        pieces = []
        for source, (steps, parts) in zip(sources, plan):
            rows, width = source.shape
            cut = source.reshape(rows, width // (team * depth), team, depth)
            for step in range(steps):
                share = lax.dynamic_index_in_dim(cut, info[0] ^ step, 2, keepdims=False)
                pieces += jnp.split(share.reshape(rows, -1), parts, axis=1)
    out = []
    for steps, parts in plan:
        out.append([[pieces.pop(0) for _ in range(parts)] for _ in range(steps)])
    return out


def reach_tables(rate, coef, reach, decay8):
    order = rate.shape[0]
    step = lax.broadcasted_iota(jnp.int32, (8, LANES), 0).astype(f32) + 1.0
    for k in range(order):
        reach[k] = coef[k : k + 1] * jnp.exp(-step * rate[k : k + 1])
        decay8[k] = jnp.exp(jnp.broadcast_to(-8.0 * rate[k : k + 1], (8, LANES)))


def local_kernel(info_ref, *refs):
    values = refs[:TEAM]
    rate_ref, coef_ref, skip_ref, y_ref, end_ref, wide, taps, reach, decay8, start = refs[TEAM:]
    me = info_ref[0]
    order = rate_ref.shape[0]
    rows = values[0].shape[0]
    per = rows // BLOCK
    wide[:, :BLOCK, :] = jnp.zeros((wide.shape[0], BLOCK, LANES), f32)

    @pl.loop(0, rate_ref.shape[1] // LANES)
    def _(tile):
        lanes = pl.ds(pl.multiple_of(tile * LANES, LANES), LANES)
        for step in range(TEAM):
            for b in range(per):
                wide[(me ^ step) * per + b, BLOCK:, :] = values[step][
                    b * BLOCK : (b + 1) * BLOCK, lanes
                ].astype(f32)
        rate, coef, skip = rate_ref[:, lanes], coef_ref[:, lanes], skip_ref[:, lanes]
        lam = jnp.exp(-rate)
        power = coef
        for t in range(BLOCK):
            tap = jnp.sum(power, axis=0, keepdims=True).astype(bf16).astype(f32)
            taps[t] = jnp.broadcast_to(tap, (8, LANES))
            power = power * lam
        reach_tables(rate, coef, reach, decay8)
        lam8 = jnp.exp(-8.0 * rate)

        def block(b, state):
            start[...] = state
            y = [skip * wide[b, BLOCK + 8 * i : BLOCK + 8 * i + 8, :] for i in range(BLOCK // 8)]
            for t in range(BLOCK):
                tap = taps[t]
                for i in range(t // 8, BLOCK // 8):
                    at = BLOCK + 8 * i - t
                    y[i] = y[i] + tap * wide[b, at : at + 8, :]
            for k in range(order):
                term = reach[k] * start[k : k + 1, :]
                decay = decay8[k]
                for i in range(BLOCK // 8):
                    y[i] = y[i] + term
                    if i + 1 < BLOCK // 8:
                        term = term * decay
            for i in range(BLOCK // 8):
                y_ref[tile, pl.ds(pl.multiple_of(b * BLOCK + 8 * i, 8), 8), :] = y[i]
            for i in range(BLOCK // 8):
                at = BLOCK + 8 * i
                inflow = jnp.broadcast_to(wide[b, at : at + 1, :], (order, LANES))
                for t in range(1, 8):
                    inflow = lam * inflow + wide[b, at + t : at + t + 1, :]
                state = lam8 * state + inflow
            return state

        end_ref[:, lanes] = lax.fori_loop(0, TEAM * per, block, jnp.zeros((order, LANES), f32))


def gate_kernel(gaps, info_ref, *refs):
    gates = refs[:TEAM]
    y_refs = refs[TEAM : TEAM + 2]
    rate_ref, coef_ref, near_ref = refs[TEAM + 2 : TEAM + 5]
    far = refs[TEAM + 5 : TEAM + 5 + gaps]
    out_ref, reach, decay8, start = refs[TEAM + 5 + gaps :]
    me, high = info_ref[0], info_ref[1]
    order = rate_ref.shape[0]
    rows = gates[0].shape[0]
    span = float(TEAM * rows)

    def gate_tile(y_ref, tile, row):
        lanes = pl.ds(pl.multiple_of(tile * LANES, LANES), LANES)
        rate, coef = rate_ref[:, lanes], coef_ref[:, lanes]
        reach_tables(rate, coef, reach, decay8)
        state = jnp.zeros((order, LANES), f32)
        for gap in range(gaps):
            state = state + jnp.exp(-2.0 * span * gap * rate) * far[gap][:, lanes]
        after = jnp.exp(-span * rate) * state + near_ref[:, lanes]
        state = jnp.where(high == 1, after, state)
        for step in range(TEAM):
            place = me ^ step
            start[...] = state * jnp.exp(-(rows * place).astype(f32) * rate)
            terms = [reach[k] * start[k : k + 1, :] for k in range(order)]
            goes = place ^ (me & 2)
            for at in range(0, rows, 16):
                halves = []
                for half in range(2):
                    total = list(terms)
                    while len(total) > 1:
                        total = [a + b for a, b in zip(total[::2], total[1::2])]
                    here = pl.multiple_of(place * rows + at + 8 * half, 8)
                    halves.append(total[0] + y_ref[row, pl.ds(here, 8), :])
                    terms = [term * decay8[k] for k, term in enumerate(terms)]
                conv = jnp.concatenate(halves, axis=0)
                gated = gates[step][at : at + 16, lanes].astype(f32) * conv
                out_ref[tile, pl.ds(pl.multiple_of(goes * rows + at, 16), 16), :] = gated.astype(bf16)

    for part, y_ref in enumerate(y_refs):
        tiles = y_ref.shape[0]

        @pl.loop(0, tiles)
        def _(row, y_ref=y_ref, first=part * tiles):
            gate_tile(y_ref, first + row, row)


def product(groups, gated_ref, weights):
    total = None
    for pair, rows in enumerate(weights):
        first, second = groups[2 * pair], groups[2 * pair + 1]
        left = jnp.concatenate([gated_ref[first], gated_ref[second]], axis=1)
        right = jnp.concatenate([ref[...] for ref in rows], axis=0)
        term = jnp.dot(left, right, preferred_element_type=f32)
        total = term if total is None else total + term
    return total


def pairs_of(flat, sizes):
    flat, out = list(flat), []
    for size in sizes:
        out.append([flat.pop(0) for _ in range(size)])
    return out


def own_product_kernel(sizes, info_ref, gated_ref, *refs):
    groups = [info_ref[3 + slot] for slot in range(2 * len(sizes))]
    weights, out = pairs_of(refs[:-1], sizes), refs[-1]
    wide = out.shape[1]
    step = min(wide, 256)
    for at in range(0, wide, step):
        part = [[ref.at[:, at : at + step] for ref in rows] for rows in weights]
        out[:, at : at + step] = product(groups, gated_ref, part)


def project_kernel(sizes, at, info_ref, gated_ref, own_ref, *refs):
    groups = [info_ref[3 + slot] for slot in range(2 * len(sizes))]
    weights, outs, total = pairs_of(refs[: sum(sizes)], sizes), refs[sum(sizes) : -1], refs[-1]
    core = info_ref[2]
    rows, wide = outs[0].shape
    total[...] = own_ref[:, at : at + wide] + product(groups, gated_ref, weights)
    for step, out in enumerate(outs):
        start = (step // 2) * 2 * rows + (core ^ (step & 1)) * rows
        out[...] = total[pl.ds(pl.multiple_of(start, rows), rows), :].astype(out.dtype)


def finish_kernel(parts, info_ref, *refs):
    core = info_ref[2]
    out_ref = refs[-1]
    half = out_ref.shape[1] // 2
    at = 0
    for part in range(parts):
        mine, his, mine_far, his_far = refs[4 * part : 4 * part + 4]
        wide = mine.shape[1]
        near = pl.ds(pl.multiple_of(core * half + at, LANES), wide)
        away = pl.ds(pl.multiple_of((1 - core) * half + at, LANES), wide)
        out_ref[:, near] = (mine[...] + mine_far[...].astype(f32)).astype(bf16)
        out_ref[:, away] = (his[...].astype(f32) + his_far[...].astype(f32)).astype(bf16)
        at += wide


def halves_kernel(cut, info_ref, weight_ref, keep_ref, *give_refs):
    core = info_ref[2]
    half = keep_ref.shape[1]
    keep_ref[...] = weight_ref[:, pl.ds(pl.multiple_of(core * half, LANES), half)]
    at = 0
    for give_ref in give_refs:
        wide = give_ref.shape[1]
        start = pl.multiple_of((1 - core) * half + at, LANES)
        give_ref[...] = weight_ref[:, pl.ds(start, wide)]
        at += wide


def on_device(q_gate, values_in, decay_rate, residue, skip_gain, out_weight):
    rows, width = q_gate.shape
    depth, features = out_weight.shape
    order = decay_rate.shape[1]
    count = lax.axis_size("seq")
    heights = count // (2 * TEAM)
    mine = lax.axis_index("seq")
    me, core = mine % TEAM, mine % 2
    y, z = (mine // TEAM) % 2, mine // (2 * TEAM)
    share = width // TEAM
    half = features // 2
    parts = 2

    def swap(value, bit):
        return lax.ppermute(value, "seq", [(i, i ^ bit) for i in range(count)])

    def up(value, gap, wrap):
        hop = gap * 2 * TEAM
        pairs = [(i, (i + hop) % count) for i in range(count) if wrap or i + hop < count]
        return lax.ppermute(value, "seq", pairs)

    groups = []
    for gap in range(heights):
        at = (z - gap) % heights
        groups += [at * 2 + y, at * 2 + (1 - y)]
    info = jnp.stack([me, y, core] + groups).astype(jnp.int32)

    (values,) = split_channels(info, TEAM, depth, [values_in], [(TEAM, parts)])
    values = [values[0]] + [[swap(part, s) for part in values[s]] for s in range(1, TEAM)]

    cut = half * FIRST // 8
    keep, give0, give1 = call(
        functools.partial(halves_kernel, cut),
        [
            jax.ShapeDtypeStruct((depth, half), bf16),
            jax.ShapeDtypeStruct((depth, cut), bf16),
            jax.ShapeDtypeStruct((depth, half - cut), bf16),
        ],
    )(info, out_weight)

    def along_first(held):
        slots = [[held, swap(held, TEAM)]]
        for _ in range(1, heights):
            held = up(held, 1, True)
            slots.append([held, swap(held, TEAM)])
        return slots

    def across_first(held):
        held = jnp.concatenate([held, swap(held, TEAM)], axis=0)
        slots = [[held]]
        for _ in range(1, heights):
            held = up(held, 1, True)
            slots.append([held])
        return slots

    own_rows = along_first(keep)
    other_rows = [along_first(swap(give0, 1)), across_first(swap(give1, 1))]

    gates, rates, residues, skip = split_channels(
        info,
        TEAM,
        depth,
        [q_gate, decay_rate.T, residue.T, skip_gain[None]],
        [(TEAM, 1), (1, 1), (1, 1), (1, 1)],
    )
    gates = [gates[0][0]] + [swap(gates[step][0], step) for step in range(1, TEAM)]
    rates, residues, skip = rates[0][0], residues[0][0], skip[0][0]
    coef = residues * jnp.sqrt(-jnp.expm1(-2.0 * rates))

    tiles = share // LANES
    blocks = TEAM * rows // BLOCK
    waits = [
        [own_rows[1][0]],
        [own_rows[min(2, heights - 1)][0], other_rows[0][1][0], own_rows[0][1], other_rows[1][0][0]],
    ]
    y_local, ends = [], []
    for part in range(parts):
        lanes = slice(part * share // parts, (part + 1) * share // parts)
        y_part, end = call(
            local_kernel,
            [
                jax.ShapeDtypeStruct((tiles // parts, TEAM * rows, LANES), f32),
                jax.ShapeDtypeStruct((order, share // parts), f32),
            ],
            [
                pltpu.VMEM((blocks, 2 * BLOCK, LANES), f32),
                pltpu.VMEM((BLOCK, 8, LANES), f32),
                pltpu.VMEM((order, 8, LANES), f32),
                pltpu.VMEM((order, 8, LANES), f32),
                pltpu.VMEM((order, LANES), f32),
            ],
            after=waits[part],
        )(info, *[v[part] for v in values], rates[:, lanes], coef[:, lanes], skip[:, lanes])
        y_local.append(y_part)
        ends.append(end)
    end = jnp.concatenate(ends, axis=1)

    near = swap(end, TEAM)
    first, second = jnp.where(y == 0, end, near), jnp.where(y == 0, near, end)
    pair_end = jnp.exp(-float(TEAM * rows) * rates) * first + second
    far = [up(pair_end, gap, False) for gap in range(1, heights)]
    gated = call(
        functools.partial(gate_kernel, heights - 1),
        jax.ShapeDtypeStruct((tiles, TEAM * rows, LANES), bf16),
        [
            pltpu.VMEM((order, 8, LANES), f32),
            pltpu.VMEM((order, 8, LANES), f32),
            pltpu.VMEM((order, LANES), f32),
        ],
        after=[
            other_rows[0][min(2, heights - 1)][0],
            other_rows[1][1][0],
            own_rows[1][1],
            other_rows[0][1][1],
        ],
    )(info, *gates, *y_local, rates, coef, near, *far)
    other = swap(gated, 1)

    if depth % LANES:
        runs = width // (TEAM * depth)

        def by_group(value):
            value = value.transpose(1, 0, 2).reshape(TEAM * rows, runs, depth)
            return value.transpose(1, 0, 2)

        gated, other = by_group(gated), by_group(other)

    def laid_out(slots):
        return [len(pair) for pair in slots], [ref for pair in slots for ref in pair]

    sizes, flat = laid_out(own_rows)
    own = call(
        functools.partial(own_product_kernel, sizes),
        jax.ShapeDtypeStruct((TEAM * rows, half), f32),
    )(info, gated, *flat)
    finished, at = [], 0
    for slots in other_rows:
        sizes, flat = laid_out(slots)
        wide = flat[0].shape[1]
        shape = functools.partial(jax.ShapeDtypeStruct, (rows, wide))
        sums = call(
            functools.partial(project_kernel, sizes, at),
            [shape(f32), shape(f32), shape(bf16), shape(bf16)],
            [pltpu.VMEM((TEAM * rows, wide), f32)],
        )(info, other, own, *flat)
        finished += [sums[0]] + [swap(sums[step], step) for step in range(1, TEAM)]
        at += wide
    return call(
        functools.partial(finish_kernel, len(other_rows)),
        jax.ShapeDtypeStruct((rows, features), bf16),
    )(info, *finished)


def solution(mesh):
    in_specs = (
        P(("groups", "seq"), None),
        P(("groups", "seq"), None),
        P(),
        P(),
        P(),
        P("seq", None),
    )
    out_specs = P(("groups", "seq"), None)
    return jax.shard_map(
        on_device, mesh=mesh, in_specs=in_specs, out_specs=out_specs, check_vma=False
    )
```

```python
import functools

import jax
import jax.numpy as jnp
from jax import lax
from jax.experimental import pallas as pl
from jax.experimental.pallas import tpu as pltpu
from jax.sharding import PartitionSpec as P

BLOCK = 32
LANES = 128
TEAM = 4
LAST_PARTS = 2
VMEM_LIMIT = 32 * 1024 * 1024

f32 = jnp.float32
bf16 = jnp.bfloat16


def call(kernel, out_shape, scratch=(), after=()):
    def body(*refs):
        return kernel(*refs[len(after) :])

    def run(info, *args):
        return pl.pallas_call(
            body,
            out_shape=out_shape,
            in_specs=[pl.BlockSpec(memory_space=pl.ANY)] * len(after)
            + [pl.BlockSpec(memory_space=pltpu.SMEM)]
            + [pl.BlockSpec()] * len(args),
            scratch_shapes=list(scratch),
            compiler_params=pltpu.CompilerParams(vmem_limit_bytes=VMEM_LIMIT),
            cost_estimate=pl.CostEstimate(flops=0, bytes_accessed=0, transcendentals=0),
        )(*after, info, *args)

    return run


def halves_kernel(info_ref, weight_ref, give_ref, held_ref, sems):
    core = info_ref[2]
    depth, half = give_ref.shape
    copies = []
    for which, out in enumerate((give_ref, held_ref.at[:depth])):
        at = pl.multiple_of((core ^ (1 - which)) * half, LANES)
        copies.append(
            pltpu.make_async_copy(weight_ref.at[:, pl.ds(at, half)], out, sems.at[which])
        )
        copies[-1].start()
    for copy in copies:
        copy.wait()


def halves_of(info, weight):
    depth, half = weight.shape[0], weight.shape[1] // 2
    return pl.pallas_call(
        halves_kernel,
        out_shape=[
            jax.ShapeDtypeStruct((depth, half), weight.dtype),
            jax.ShapeDtypeStruct((2 * depth, half), weight.dtype),
        ],
        in_specs=[
            pl.BlockSpec(memory_space=pltpu.SMEM),
            pl.BlockSpec(memory_space=pltpu.HBM),
        ],
        out_specs=[pl.BlockSpec(memory_space=pltpu.VMEM)] * 2,
        scratch_shapes=[pltpu.SemaphoreType.DMA((2,))],
    )(info, weight)


CHUNKS = 4


def deal_kernel(team, depth, plan, info_ref, *refs):
    me = info_ref[0]
    count = len(plan)
    sources, held, sems = refs[:count], refs[-1 - count : -1], refs[-1]
    outs = list(refs[count : -1 - count])
    copies = []
    for source, whole in zip(sources, held):
        wide = source.shape[1] // CHUNKS
        for chunk in range(CHUNKS):
            cols = slice(chunk * wide, (chunk + 1) * wide)
            sem = sems.at[len(copies)]
            copies.append(pltpu.make_async_copy(source.at[:, cols], whole.at[:, cols], sem))
            copies[-1].start()
    for source, whole, steps in zip(sources, held, plan):
        rows = source.shape[0]
        runs = source.shape[1] // (team * depth)
        mine = [outs.pop(0) for _ in range(min(steps, 3))]
        for run in range(runs):
            if run % (runs // CHUNKS) == 0:
                copies.pop(0).wait()
            for step in range(steps):
                here = slice(rows * (step == 3), rows * (step == 3) + rows)
                at = pl.multiple_of((run * team + (me ^ step)) * depth, depth)
                mine[min(step, 2)][here, run * depth : (run + 1) * depth] = whole[:, pl.ds(at, depth)]


def deal(info, team, depth, sources, plan):
    pieces = []
    if depth % LANES == 0:
        shapes = []
        for source, steps in zip(sources, plan):
            rows, share = source.shape[0], source.shape[1] // team
            for deep in [rows, rows, 2 * rows][:steps]:
                shapes.append(jax.ShapeDtypeStruct((deep, share), source.dtype))
        pieces = list(
            pl.pallas_call(
                functools.partial(deal_kernel, team, depth, plan),
                out_shape=shapes,
                in_specs=[pl.BlockSpec(memory_space=pltpu.SMEM)]
                + [pl.BlockSpec(memory_space=pltpu.HBM)] * len(sources),
                out_specs=[pl.BlockSpec(memory_space=pltpu.VMEM)] * len(shapes),
                scratch_shapes=[pltpu.VMEM(source.shape, source.dtype) for source in sources]
                + [pltpu.SemaphoreType.DMA((CHUNKS * len(sources),))],
                compiler_params=pltpu.CompilerParams(vmem_limit_bytes=VMEM_LIMIT),
            )(info, *sources)
        )
    else:
        for source, steps in zip(sources, plan):
            rows, width = source.shape
            cut = source.reshape(rows, width // (team * depth), team, depth)
            shares = []
            for step in range(steps):
                share = lax.dynamic_index_in_dim(cut, info[0] ^ step, 2, keepdims=False)
                shares.append(share.reshape(rows, -1))
            if steps == team:
                shares[2:] = [jnp.concatenate(shares[2:], axis=0)]
            pieces += shares
    return [[pieces.pop(0) for _ in range(min(steps, 3))] for steps in plan]


def by_step(parts):
    rows = parts[0].shape[0]
    return [parts[0], parts[1], parts[2].at[:rows], parts[3].at[rows:]]


def spread(values, me, lanes, wide, above):
    per = values[0].shape[0] // BLOCK
    for step in range(TEAM):
        for b in range(per):
            rows = values[step][b * BLOCK : (b + 1) * BLOCK, lanes].astype(f32)
            wide[(me ^ step) * per + b, above:, :] = rows


def tile_lanes(info_ref, slot):
    return pl.ds(pl.multiple_of(info_ref[3 + slot] * LANES, LANES), LANES)


def state_kernel(info_ref, *refs):
    values = by_step(refs[:TEAM])
    rate_ref, starts_ref, end_ref, wide = refs[TEAM:]
    order = rate_ref.shape[0]
    me = info_ref[0]

    @pl.loop(0, starts_ref.shape[0])
    def _(slot):
        lanes = tile_lanes(info_ref, slot)
        spread(values, me, lanes, wide, 0)
        rate = rate_ref[:, lanes]
        lam, lam8 = jnp.exp(-rate), jnp.exp(-8.0 * rate)

        def block(b, state):
            starts_ref[slot, b] = state
            for at in range(0, BLOCK, 8):
                inflow = jnp.broadcast_to(wide[b, at : at + 1, :], (order, LANES))
                for t in range(1, 8):
                    inflow = lam * inflow + wide[b, at + t : at + t + 1, :]
                state = lam8 * state + inflow
            return state

        end_ref[:, lanes] = lax.fori_loop(0, wide.shape[0], block, jnp.zeros((order, LANES), f32))


def taps_kernel(base, info_ref, *refs):
    values = by_step(refs[:TEAM])
    rate_ref, coef_ref, skip_ref, y_ref, wide, taps = refs[TEAM:]
    me = info_ref[0]
    wide[:, :BLOCK, :] = jnp.zeros((wide.shape[0], BLOCK, LANES), f32)

    @pl.loop(0, y_ref.shape[0])
    def _(slot):
        lanes = tile_lanes(info_ref, base + slot)
        spread(values, me, lanes, wide, BLOCK)
        skip = skip_ref[:, lanes]
        lam = jnp.exp(-rate_ref[:, lanes])
        power = coef_ref[:, lanes]
        for t in range(BLOCK):
            tap = jnp.sum(power, axis=0, keepdims=True).astype(bf16).astype(f32)
            taps[t] = jnp.broadcast_to(tap, (8, LANES))
            power = power * lam

        @pl.loop(0, wide.shape[0])
        def _(b):
            y = [skip * wide[b, BLOCK + 8 * i : BLOCK + 8 * i + 8, :] for i in range(BLOCK // 8)]
            for t in range(BLOCK):
                tap = taps[t]
                for i in range(t // 8, BLOCK // 8):
                    at = BLOCK + 8 * i - t
                    y[i] = y[i] + tap * wide[b, at : at + 8, :]
            for i in range(BLOCK // 8):
                y_ref[slot, pl.ds(pl.multiple_of(b * BLOCK + 8 * i, 8), 8), :] = y[i]


def gate_kernel(base, reaches, info_ref, *refs):
    gaps = len(reaches)
    gates = by_step(refs[:TEAM])
    y_ref, starts_ref, rate_ref, coef_ref, near_ref = refs[TEAM : TEAM + 5]
    far = refs[TEAM + 5 : TEAM + 5 + gaps]
    out_ref, reach, decay8, start = refs[TEAM + 5 + gaps :]
    me, high = info_ref[0], info_ref[1]
    order = rate_ref.shape[0]
    rows = gates[0].shape[0]
    per = rows // BLOCK
    span = float(TEAM * rows)
    ahead = lax.broadcasted_iota(jnp.int32, (8, LANES), 0).astype(f32) + 1.0

    @pl.loop(0, y_ref.shape[0])
    def _(slot):
        lanes = tile_lanes(info_ref, base + slot)
        rate, coef = rate_ref[:, lanes], coef_ref[:, lanes]
        for k in range(order):
            reach[k] = coef[k : k + 1] * jnp.exp(-ahead * rate[k : k + 1])
            decay8[k] = jnp.exp(jnp.broadcast_to(-8.0 * rate[k : k + 1], (8, LANES)))
        state = jnp.zeros((order, LANES), f32)
        for gap, ref in zip(reaches, far):
            state = state + jnp.exp(-2.0 * span * gap * rate) * ref[:, lanes]
        after = jnp.exp(-span * rate) * state + near_ref[:, lanes]
        state = jnp.where(high == 1, after, state)
        over = jnp.exp(-float(BLOCK) * rate)
        for step in range(TEAM):
            place = me ^ step
            goes = place ^ (me & 2)
            entering = state * jnp.exp(-(rows * place).astype(f32) * rate)
            for b in range(per):
                start[b] = starts_ref[base + slot, place * per + b] + entering
                entering = entering * over
            for b in range(per):
                y = []
                for i in range(BLOCK // 8):
                    here = pl.multiple_of(place * rows + b * BLOCK + 8 * i, 8)
                    y.append(y_ref[slot, pl.ds(here, 8), :])
                for k in range(order):
                    term = reach[k] * start[b, k : k + 1, :]
                    decay = decay8[k]
                    for i in range(BLOCK // 8):
                        y[i] = y[i] + term
                        if i + 1 < BLOCK // 8:
                            term = term * decay
                for i in range(0, BLOCK // 8, 2):
                    at = b * BLOCK + 8 * i
                    conv = jnp.concatenate(y[i : i + 2], axis=0)
                    gated = gates[step][at : at + 16, lanes].astype(f32) * conv
                    to = pl.ds(pl.multiple_of(goes * rows + at, 16), 16)
                    out_ref[slot, to, :] = gated.astype(bf16)


def gated_columns(gated, halves, per, group):
    own, other = (gated[2 * (group // per) + i][group % per] for i in range(2))
    return jnp.concatenate([own, other], axis=1)


def early_kernel(halves, in_slots, info_ref, *refs):
    gated, weights, out = refs[: 2 * halves], refs[2 * halves : -1], refs[-1]
    per = gated[0].shape[0]
    wide = out.shape[1]
    step = min(wide, 256)
    for slot, weight in enumerate(weights):
        if in_slots:
            left = gated_columns(gated, halves, per, slot)
        else:
            left = jnp.concatenate([ref[info_ref[3 + slot]] for ref in gated], axis=1)
        for col in range(0, wide, step):
            cols = slice(col, col + step)
            term = jnp.dot(left, weight[:, cols], preferred_element_type=f32)
            out[:, cols] = term if slot == 0 else out[:, cols] + term


def project_kernel(halves, in_slots, slots, at, info_ref, *refs):
    gated, (early_ref, near_ref, away_ref) = refs[: 2 * halves], refs[2 * halves : 2 * halves + 3]
    outs, total = refs[2 * halves + 3 : -1], refs[-1]
    core = info_ref[2]
    per = gated[0].shape[0]
    rows, wide = outs[0].shape
    step = min(wide, 256)
    lefts = []
    for slot in (slots - 2, slots - 1):
        if in_slots:
            lefts.append(gated_columns(gated, halves, per, slot))
        else:
            lefts.append(jnp.concatenate([ref[info_ref[3 + slot]] for ref in gated], axis=1))
    for col in range(0, wide, step):
        term = early_ref[:, at + col : at + col + step]
        term += jnp.dot(lefts[0], near_ref[:, at + col : at + col + step], preferred_element_type=f32)
        term += jnp.dot(lefts[1], away_ref[:, col : col + step], preferred_element_type=f32)
        total[:, col : col + step] = term
    for step, out in enumerate(outs):
        start = (step // 2) * 2 * rows + (core ^ (step & 1)) * rows
        out[...] = total[pl.ds(pl.multiple_of(start, rows), rows), :].astype(out.dtype)


def finish_kernel(parts, info_ref, *refs):
    core = info_ref[2]
    out_ref = refs[-1]
    half = out_ref.shape[1] // 2
    at = 0
    for part in range(parts):
        mine, his, mine_far, his_far = refs[4 * part : 4 * part + 4]
        wide = mine.shape[1]
        near = pl.ds(pl.multiple_of(core * half + at, LANES), wide)
        away = pl.ds(pl.multiple_of((1 - core) * half + at, LANES), wide)
        out_ref[:, near] = (mine[...] + mine_far[...].astype(f32)).astype(bf16)
        out_ref[:, away] = (his[...].astype(f32) + his_far[...].astype(f32)).astype(bf16)
        at += wide


def on_device(q_gate, values_in, decay_rate, residue, skip_gain, out_weight):
    rows, width = q_gate.shape
    depth, features = out_weight.shape
    order = decay_rate.shape[1]
    count = lax.axis_size("seq")
    heights = count // (2 * TEAM)
    mine = lax.axis_index("seq")
    me, core = mine % TEAM, mine % 2
    y, z = (mine // TEAM) % 2, mine // (2 * TEAM)
    share = width // TEAM
    half = features // 2

    def swap(value, bit):
        return lax.ppermute(value, "seq", [(i, i ^ bit) for i in range(count)])

    def up(value, gap, wrap):
        hop = gap * 2 * TEAM
        pairs = [(i, (i + hop) % count) for i in range(count) if wrap or i + hop < count]
        return lax.ppermute(value, "seq", pairs)

    in_slots = depth % LANES == 0
    groups = []
    for gap in range(heights):
        at = (z - gap) % heights
        groups += [at * 2 + y, at * 2 + (1 - y)]
    tiles = share // LANES
    order_of = groups if in_slots else list(range(tiles))
    info = jnp.stack([jnp.int32(n) for n in [me, y, core] + order_of])
    group_info = info if in_slots else jnp.stack([jnp.int32(n) for n in [me, y, core] + groups])

    def share_out(shares):
        across = swap(shares[2], 2)
        return [shares[0], swap(shares[1], 1), across, swap(across, 1)]

    def share_out(shares):
        across = swap(shares[2], 2)
        return [shares[0], swap(shares[1], 1), across, swap(across, 1)]

    def tied(value, *others):
        return lax.optimization_barrier((value, *others))[0]

    give, held = halves_of(info, out_weight)
    held = lax.dynamic_update_slice(held, swap(give, 1), (depth, 0))
    last = heights - 1
    weights, weights_away = [held], []
    for gap in range(last):
        weights_away.append(swap(weights[gap], TEAM))
        weights.append(up(weights[gap], 1, True))
    wide = half // LAST_PARTS
    finals = [
        swap(weights[last][:, part * wide : (part + 1) * wide], TEAM) for part in range(LAST_PARTS)
    ]

    (values,) = deal(info, TEAM, depth, [values_in], [TEAM])
    values = share_out(values)
    gates, rates, residues, skip = deal(
        info, TEAM, depth, [q_gate, decay_rate.T, residue.T, skip_gain[None]], [TEAM, 1, 1, 1]
    )
    gates[2] = tied(gates[2], values[2])
    gates = share_out(gates)
    rates, residues, skip = rates[0], residues[0], skip[0]
    coef = residues * jnp.sqrt(-jnp.expm1(-2.0 * rates))

    blocks = TEAM * rows // BLOCK
    starts, end = call(
        state_kernel,
        [
            jax.ShapeDtypeStruct((tiles, blocks, order, LANES), f32),
            jax.ShapeDtypeStruct((order, share), f32),
        ],
        [pltpu.VMEM((blocks, BLOCK, LANES), f32)],
        after=[weights[min(1, last)], weights_away[0]],
    )(info, *values, rates)

    pieces = 4
    some = tiles // pieces
    local = [
        call(
            functools.partial(taps_kernel, part * some),
            jax.ShapeDtypeStruct((some, TEAM * rows, LANES), f32),
            [pltpu.VMEM((blocks, 2 * BLOCK, LANES), f32), pltpu.VMEM((BLOCK, 8, LANES), f32)],
            after=[end],
        )(info, *values, rates, coef, skip)
        for part in range(pieces)
    ]

    near = swap(end, TEAM)
    first, second = jnp.where(y == 0, end, near), jnp.where(y == 0, near, end)
    span = float(TEAM * rows)
    held = jnp.exp(-span * rates) * first + second
    far, gap, part = [], 1, 0
    while gap < heights:
        held = tied(held, local[min(part, pieces - 1)])
        far.append((gap - 1, up(held, gap, False)))
        held = held + jnp.exp(-2.0 * span * gap * rates) * far[-1][1]
        gap, part = gap * 2, part + 1

    tables = [pltpu.VMEM((order, 8, LANES), f32)] * 2
    gated = [
        call(
            functools.partial(gate_kernel, part * some, [lag for lag, _ in far]),
            jax.ShapeDtypeStruct((some, TEAM * rows, LANES), bf16),
            tables + [pltpu.VMEM((rows // BLOCK, order, LANES), f32)],
            after=[weights_away[min(1, last - 1)], weights[min(2, last)]] if part == 0 else [],
        )(info, *gates, local[part], starts, rates, coef, near, *[state for _, state in far])
        for part in range(pieces)
    ]
    if in_slots:
        gated = [ref for part in gated for ref in (part, swap(part, 1))]
    else:
        gated = jnp.concatenate(gated, axis=0).transpose(1, 0, 2)
        gated = gated.reshape(TEAM * rows, width // (TEAM * depth), depth).transpose(1, 0, 2)
        gated = [gated, swap(gated, 1)]
    halves = len(gated) // 2

    blocks_early = [ref for gap in range(last) for ref in (weights[gap], weights_away[gap])]
    early = call(
        functools.partial(early_kernel, halves, in_slots),
        jax.ShapeDtypeStruct((TEAM * rows, half), f32),
    )(group_info, *gated, *blocks_early)
    finished = []
    for part, final in enumerate(finals):
        shape = functools.partial(jax.ShapeDtypeStruct, (rows, wide))
        sums = call(
            functools.partial(project_kernel, halves, in_slots, 2 * heights, part * wide),
            [shape(f32), shape(f32), shape(bf16), shape(bf16)],
            [pltpu.VMEM((TEAM * rows, wide), f32)],
        )(group_info, *gated, early, weights[last], final)
        finished += [sums[0]] + [swap(sums[step], step) for step in range(1, TEAM)]
    return call(
        functools.partial(finish_kernel, LAST_PARTS),
        jax.ShapeDtypeStruct((rows, features), bf16),
    )(info, *finished)


def solution(mesh):
    in_specs = (
        P(("groups", "seq"), None),
        P(("groups", "seq"), None),
        P(),
        P(),
        P(),
        P("seq", None),
    )
    out_specs = P(("groups", "seq"), None)
    return jax.shard_map(
        on_device, mesh=mesh, in_specs=in_specs, out_specs=out_specs, check_vma=False
    )
```

```python
import functools

import jax
import jax.numpy as jnp
from jax import lax
from jax.experimental import pallas as pl
from jax.experimental.pallas import tpu as pltpu
from jax.sharding import PartitionSpec as P

BLOCK = 32
LANES = 128
CHUNKS = 8
TEAM = 4
LAST_PARTS = 2
VMEM_LIMIT = 8 * 1024 * 1024

f32 = jnp.float32
bf16 = jnp.bfloat16


def tied(value, *others):
    return lax.optimization_barrier((value, *others))[0]


def call(kernel, out_shape, scratch=(), after=(), micros=0.0):
    def run(info, *args):
        return pl.pallas_call(
            kernel,
            out_shape=out_shape,
            in_specs=[pl.BlockSpec(memory_space=pltpu.SMEM)] + [pl.BlockSpec()] * len(args),
            scratch_shapes=list(scratch),
            compiler_params=pltpu.CompilerParams(vmem_limit_bytes=VMEM_LIMIT),
            cost_estimate=pl.CostEstimate(
                flops=int(micros * 1.1e9), bytes_accessed=int(micros * 3.6e6), transcendentals=0
            ),
        )(tied(info, *after), *args)

    return run


def deal_kernel(team, depth, plan, info_ref, *refs):
    me = info_ref[0]
    count = len(plan)
    sources, held, sems = refs[:count], refs[-1 - count : -1], refs[-1]
    outs = list(refs[count : -1 - count])
    copies = []
    for source, whole in zip(sources, held):
        wide = source.shape[1] // CHUNKS
        for chunk in range(CHUNKS):
            cols = slice(chunk * wide, (chunk + 1) * wide)
            sem = sems.at[len(copies)]
            copies.append(pltpu.make_async_copy(source.at[:, cols], whole.at[:, cols], sem))
            copies[-1].start()
    for source, whole, steps in zip(sources, held, plan):
        runs = source.shape[1] // (team * depth)
        mine = [outs.pop(0) for _ in range(steps)]
        for run in range(runs):
            if run % (runs // CHUNKS) == 0:
                copies.pop(0).wait()
            for step in range(steps):
                at = pl.multiple_of((run * team + (me ^ step)) * depth, depth)
                mine[step][:, run * depth : (run + 1) * depth] = whole[:, pl.ds(at, depth)]


def deal(info, team, depth, sources, plan):
    pieces = []
    if depth % LANES == 0:
        shapes = []
        for source, steps in zip(sources, plan):
            share = (source.shape[0], source.shape[1] // team)
            shapes += [jax.ShapeDtypeStruct(share, source.dtype)] * steps
        pieces = list(
            pl.pallas_call(
                functools.partial(deal_kernel, team, depth, plan),
                out_shape=shapes,
                in_specs=[pl.BlockSpec(memory_space=pltpu.SMEM)]
                + [pl.BlockSpec(memory_space=pltpu.HBM)] * len(sources),
                out_specs=[pl.BlockSpec(memory_space=pltpu.VMEM)] * len(shapes),
                scratch_shapes=[pltpu.VMEM(source.shape, source.dtype) for source in sources]
                + [pltpu.SemaphoreType.DMA((CHUNKS * len(sources),))],
                compiler_params=pltpu.CompilerParams(vmem_limit_bytes=VMEM_LIMIT),
            )(info, *sources)
        )
    else:
        for source, steps in zip(sources, plan):
            rows, width = source.shape
            cut = source.reshape(rows, width // (team * depth), team, depth)
            for step in range(steps):
                share = lax.dynamic_index_in_dim(cut, info[0] ^ step, 2, keepdims=False)
                pieces.append(share.reshape(rows, -1))
    return [[pieces.pop(0) for _ in range(steps)] for steps in plan]


def spread(values, me, lanes, wide, above):
    per = values[0].shape[0] // BLOCK
    for step in range(TEAM):
        for b in range(per):
            rows = values[step][b * BLOCK : (b + 1) * BLOCK, lanes].astype(f32)
            wide[(me ^ step) * per + b, above:, :] = rows


def tile_lanes(info_ref, slot):
    return pl.ds(pl.multiple_of(info_ref[3 + slot] * LANES, LANES), LANES)


def state_kernel(info_ref, *refs):
    values = refs[:TEAM]
    rate_ref, starts_ref, end_ref, wide = refs[TEAM:]
    order = rate_ref.shape[0]
    me = info_ref[0]

    @pl.loop(0, starts_ref.shape[0])
    def _(slot):
        lanes = tile_lanes(info_ref, slot)
        spread(values, me, lanes, wide, 0)
        rate = rate_ref[:, lanes]
        lam, lam8 = jnp.exp(-rate), jnp.exp(-8.0 * rate)

        def block(b, state):
            starts_ref[slot, b] = state
            for at in range(0, BLOCK, 8):
                inflow = jnp.broadcast_to(wide[b, at : at + 1, :], (order, LANES))
                for t in range(1, 8):
                    inflow = lam * inflow + wide[b, at + t : at + t + 1, :]
                state = lam8 * state + inflow
            return state

        zero = jnp.zeros((order, LANES), f32)
        end_ref[:, lanes] = lax.fori_loop(0, wide.shape[0], block, zero, unroll=4)


def taps_kernel(base, info_ref, *refs):
    values = refs[:TEAM]
    rate_ref, coef_ref, skip_ref, y_ref, wide, taps = refs[TEAM:]
    me = info_ref[0]
    wide[:, :BLOCK, :] = jnp.zeros((wide.shape[0], BLOCK, LANES), f32)

    @pl.loop(0, y_ref.shape[0])
    def _(slot):
        lanes = tile_lanes(info_ref, base + slot)
        spread(values, me, lanes, wide, BLOCK)
        skip = skip_ref[:, lanes]
        lam = jnp.exp(-rate_ref[:, lanes])
        power = coef_ref[:, lanes]
        for t in range(BLOCK):
            tap = jnp.sum(power, axis=0, keepdims=True).astype(bf16).astype(f32)
            taps[t] = jnp.broadcast_to(tap, (8, LANES))
            power = power * lam

        @pl.loop(0, wide.shape[0])
        def _(b):
            y = [skip * wide[b, BLOCK + 8 * i : BLOCK + 8 * i + 8, :] for i in range(BLOCK // 8)]
            for t in range(BLOCK):
                tap = taps[t]
                for i in range(t // 8, BLOCK // 8):
                    at = BLOCK + 8 * i - t
                    y[i] = y[i] + tap * wide[b, at : at + 8, :]
            for i in range(BLOCK // 8):
                y_ref[slot, pl.ds(pl.multiple_of(b * BLOCK + 8 * i, 8), 8), :] = y[i]


def gate_kernel(base, reaches, info_ref, *refs):
    gaps = len(reaches)
    gates = refs[:TEAM]
    y_ref, starts_ref, rate_ref, coef_ref, near_ref = refs[TEAM : TEAM + 5]
    far = refs[TEAM + 5 : TEAM + 5 + gaps]
    out_ref, reach, decay8, start = refs[TEAM + 5 + gaps :]
    me, high = info_ref[0], info_ref[1]
    order = rate_ref.shape[0]
    rows = gates[0].shape[0]
    per = rows // BLOCK
    span = float(TEAM * rows)
    ahead = lax.broadcasted_iota(jnp.int32, (8, LANES), 0).astype(f32) + 1.0

    @pl.loop(0, y_ref.shape[0])
    def _(slot):
        lanes = tile_lanes(info_ref, base + slot)
        rate, coef = rate_ref[:, lanes], coef_ref[:, lanes]
        for k in range(order):
            reach[k] = coef[k : k + 1] * jnp.exp(-ahead * rate[k : k + 1])
            decay8[k] = jnp.exp(jnp.broadcast_to(-8.0 * rate[k : k + 1], (8, LANES)))
        state = jnp.zeros((order, LANES), f32)
        for gap, ref in zip(reaches, far):
            state = state + jnp.exp(-2.0 * span * gap * rate) * ref[:, lanes]
        after = jnp.exp(-span * rate) * state + near_ref[:, lanes]
        state = jnp.where(high == 1, after, state)
        over = jnp.exp(-float(BLOCK) * rate)
        for step in range(TEAM):
            place = me ^ step
            goes = place ^ (me & 2)
            entering = state * jnp.exp(-(rows * place).astype(f32) * rate)
            for b in range(per):
                start[b] = starts_ref[base + slot, place * per + b] + entering
                entering = entering * over
            for b in range(per):
                y = []
                for i in range(BLOCK // 8):
                    here = pl.multiple_of(place * rows + b * BLOCK + 8 * i, 8)
                    y.append(y_ref[slot, pl.ds(here, 8), :])
                for k in range(order):
                    term = reach[k] * start[b, k : k + 1, :]
                    decay = decay8[k]
                    for i in range(BLOCK // 8):
                        y[i] = y[i] + term
                        if i + 1 < BLOCK // 8:
                            term = term * decay
                for i in range(0, BLOCK // 8, 2):
                    at = b * BLOCK + 8 * i
                    conv = jnp.concatenate(y[i : i + 2], axis=0)
                    gated = gates[step][at : at + 16, lanes].astype(f32) * conv
                    to = pl.ds(pl.multiple_of(goes * rows + at, 16), 16)
                    out_ref[slot, to, :] = gated.astype(bf16)


def project_kernel(pieces, in_slots, at, info_ref, *refs):
    gated, weights = refs[:pieces], refs[pieces:-3]
    kept_ref, sent_ref, total = refs[-3:]
    core = info_ref[2]
    per = gated[0].shape[0]
    rows, wide = kept_ref.shape[0] // 2, kept_ref.shape[1]
    step = min(wide, 256)
    slots = len(weights)
    for slot in range(0, slots, 2):
        if in_slots:
            left = [gated[n // per][n % per] for n in (slot, slot + 1)]
        else:
            left = [gated[0][info_ref[3 + n]] for n in (slot, slot + 1)]
        left = jnp.concatenate(left, axis=1)
        for col in range(0, wide, step):
            right = []
            for ref in weights[slot : slot + 2]:
                first = col if ref.shape[1] == wide else at + col
                right.append(ref[:, first : first + step])
            term = jnp.dot(left, jnp.concatenate(right, axis=0), preferred_element_type=f32)
            cols = slice(col, col + step)
            total[:, cols] = term if slot == 0 else total[:, cols] + term
    for across in range(2):
        here = slice(across * rows, (across + 1) * rows)
        for which, out in enumerate((kept_ref, sent_ref)):
            start = (2 * across + (core ^ which)) * rows
            out[here, :] = total[pl.ds(pl.multiple_of(start, rows), rows), :].astype(out.dtype)


def join_kernel(info_ref, kept_ref, got_ref, mine_ref, away_ref):
    rows = mine_ref.shape[0]
    mine_ref[...] = kept_ref[:rows, :] + got_ref[:rows, :].astype(f32)
    away_ref[...] = (kept_ref[rows:, :] + got_ref[rows:, :].astype(f32)).astype(bf16)


def finish_kernel(info_ref, *refs):
    out_ref = refs[-1]
    at = 0
    for mine, far in zip(refs[:-1:2], refs[1:-1:2]):
        wide = mine.shape[1]
        out_ref[:, at : at + wide] = (mine[...] + far[...].astype(f32)).astype(bf16)
        at += wide


def on_device(q_gate, values_in, decay_rate, residue, skip_gain, out_weight):
    rows, width = q_gate.shape
    depth, features = out_weight.shape
    order = decay_rate.shape[1]
    count = lax.axis_size("seq")
    heights = count // (2 * TEAM)
    mine = lax.axis_index("seq")
    me, core = mine % TEAM, mine % 2
    y, z = (mine // TEAM) % 2, mine // (2 * TEAM)
    share = width // TEAM

    def swap(value, bit):
        return lax.ppermute(value, "seq", [(i, i ^ bit) for i in range(count)])

    def up(value, gap, wrap):
        hop = gap * 2 * TEAM
        pairs = [(i, (i + hop) % count) for i in range(count) if wrap or i + hop < count]
        return lax.ppermute(value, "seq", pairs)

    in_slots = depth % LANES == 0
    groups = []
    for gap in range(heights):
        at = (z - gap) % heights
        groups += [at * 2 + y, at * 2 + (1 - y)]
    tiles = share // LANES
    order_of = groups if in_slots else list(range(tiles))
    info = jnp.stack([jnp.int32(n) for n in [me, y, core] + order_of])
    group_info = info if in_slots else jnp.stack([jnp.int32(n) for n in [me, y, core] + groups])

    def share_out(shares):
        return [shares[0]] + [swap(shares[step], step) for step in range(1, TEAM)]

    def share_out(shares):
        return [shares[0]] + [swap(shares[step], step) for step in range(1, TEAM)]

    def next_round(block):
        return up(block, 1, True), swap(block, TEAM)

    last = heights - 1
    weights, weights_away = [out_weight], []
    if last > 0:
        above, away = next_round(out_weight)
        weights.append(above)
        weights_away.append(away)

    (values,) = deal(info, TEAM, depth, [values_in], [TEAM])
    values = share_out(values)
    gates, rates, residues, skip = deal(
        info, TEAM, depth, [q_gate, decay_rate.T, residue.T, skip_gain[None]], [TEAM, 1, 1, 1]
    )
    rates, residues, skip = rates[0], residues[0], skip[0]
    coef = residues * jnp.sqrt(-jnp.expm1(-2.0 * rates))
    gates = share_out(gates[:2] + [tied(gate, values[3]) for gate in gates[2:]])

    blocks = TEAM * rows // BLOCK
    starts, end = call(
        state_kernel,
        [
            jax.ShapeDtypeStruct((tiles, blocks, order, LANES), f32),
            jax.ShapeDtypeStruct((order, share), f32),
        ],
        [pltpu.VMEM((blocks, BLOCK, LANES), f32)],
        after=[weights[-1], weights_away[-1]],
        micros=0.5,
    )(info, *values, rates)

    pieces = 4
    some = tiles // pieces
    if len(weights) < heights:
        above, away = next_round(tied(weights[-1], weights_away[-1]))
        weights.append(above)
        weights_away.append(away)
    local = []
    for part in range(pieces):
        local.append(
            call(
                functools.partial(taps_kernel, part * some),
                jax.ShapeDtypeStruct((some, TEAM * rows, LANES), f32),
                [pltpu.VMEM((blocks, 2 * BLOCK, LANES), f32), pltpu.VMEM((BLOCK, 8, LANES), f32)],
                after=[end] if part == 0 else [local[-1]] + ([weights[-1], weights_away[-1]] if part > 1 else []),
                micros=0.3,
            )(info, *values, rates, coef, skip)
        )

    near = swap(end, TEAM)
    end = tied(end, local[0], local[1], *gates)
    first, second = jnp.where(y == 0, end, near), jnp.where(y == 0, near, end)
    span = float(TEAM * rows)
    held = jnp.exp(-span * rates) * first + second
    while len(weights) < heights:
        above, away = next_round(tied(weights[-1], weights_away[-1], held))
        weights.append(above)
        weights_away.append(away)
    far, gap = [], 1
    while gap < heights:
        lags = [n * gap for n in (1, 2, 3) if n * gap < heights]
        far += [(lag - 1, up(held, lag, False)) for lag in lags]
        for lag, (_, state) in zip(lags, far[-len(lags) :]):
            held = held + jnp.exp(-2.0 * span * lag * rates) * state
        gap *= 4
    wide = features // LAST_PARTS
    block = tied(weights[last], weights_away[-1])
    finals = [swap(block[:, part * wide : (part + 1) * wide], TEAM) for part in range(LAST_PARTS)]

    tables = [pltpu.VMEM((order, 8, LANES), f32)] * 2
    gated = [
        call(
            functools.partial(gate_kernel, part * some, [lag for lag, _ in far]),
            jax.ShapeDtypeStruct((some, TEAM * rows, LANES), bf16),
            tables + [pltpu.VMEM((rows // BLOCK, order, LANES), f32)],
            after=[local[-1]] if part < 2 else [weights[last], weights_away[-1]],
            micros=0.5,
        )(info, *gates, local[part], starts, rates, coef, near, *[state for _, state in far])
        for part in range(pieces)
    ]
    if not in_slots:
        gated = jnp.concatenate(gated, axis=0).transpose(1, 0, 2)
        gated = gated.reshape(TEAM * rows, width // (TEAM * depth), depth).transpose(1, 0, 2)
        gated = [gated]

    finished = []
    for part, final in enumerate(finals):
        slots = [ref for pair in zip(weights, weights_away + [final]) for ref in pair]
        kept, sent = call(
            functools.partial(project_kernel, len(gated), in_slots, part * wide),
            [jax.ShapeDtypeStruct((2 * rows, wide), dtype) for dtype in (f32, bf16)],
            [pltpu.VMEM((TEAM * rows, wide), f32)],
            micros=0.5,
        )(group_info, *gated, *slots)
        mine_sum, away_sum = call(
            join_kernel,
            [jax.ShapeDtypeStruct((rows, wide), f32), jax.ShapeDtypeStruct((rows, wide), bf16)],
        )(info, kept, swap(sent, 1))
        finished += [mine_sum, swap(away_sum, 2)]
    return call(finish_kernel, jax.ShapeDtypeStruct((rows, features), bf16))(info, *finished)


def solution(mesh):
    in_specs = (
        P(("groups", "seq"), None),
        P(("groups", "seq"), None),
        P(),
        P(),
        P(),
        P("seq", None),
    )
    out_specs = P(("groups", "seq"), None)
    return jax.shard_map(
        on_device, mesh=mesh, in_specs=in_specs, out_specs=out_specs, check_vma=False
    )
```

```python
import functools

import jax
import jax.numpy as jnp
from jax import lax
from jax.experimental import pallas as pl
from jax.experimental.pallas import tpu as pltpu
from jax.sharding import PartitionSpec as P

BLOCK = 32
LANES = 128
CHUNKS = 8
TEAM = 4
LAST_PARTS = 2
VMEM_LIMIT = 8 * 1024 * 1024

f32 = jnp.float32
bf16 = jnp.bfloat16


def tied(value, *others):
    return lax.optimization_barrier((value, *others))[0]


def call(kernel, out_shape, scratch=(), after=(), micros=0.0):
    def run(info, *args):
        return pl.pallas_call(
            kernel,
            out_shape=out_shape,
            in_specs=[pl.BlockSpec(memory_space=pltpu.SMEM)] + [pl.BlockSpec()] * len(args),
            scratch_shapes=list(scratch),
            compiler_params=pltpu.CompilerParams(vmem_limit_bytes=VMEM_LIMIT),
            cost_estimate=pl.CostEstimate(
                flops=int(micros * 1.1e9), bytes_accessed=int(micros * 3.6e6), transcendentals=0
            ),
        )(tied(info, *after), *args)

    return run


def deal_kernel(team, depth, plan, info_ref, *refs):
    me = info_ref[0]
    count = len(plan)
    sources, held, sems = refs[:count], refs[-1 - count : -1], refs[-1]
    outs = list(refs[count : -1 - count])
    copies = []
    for source, whole in zip(sources, held):
        wide = source.shape[1] // CHUNKS
        for chunk in range(CHUNKS):
            cols = slice(chunk * wide, (chunk + 1) * wide)
            sem = sems.at[len(copies)]
            copies.append(pltpu.make_async_copy(source.at[:, cols], whole.at[:, cols], sem))
            copies[-1].start()
    for source, whole, steps in zip(sources, held, plan):
        runs = source.shape[1] // (team * depth)
        mine = [outs.pop(0) for _ in range(steps)]
        for run in range(runs):
            if run % (runs // CHUNKS) == 0:
                copies.pop(0).wait()
            for step in range(steps):
                at = pl.multiple_of((run * team + (me ^ step)) * depth, depth)
                mine[step][:, run * depth : (run + 1) * depth] = whole[:, pl.ds(at, depth)]


def deal(info, team, depth, sources, plan):
    pieces = []
    if depth % LANES == 0:
        shapes = []
        for source, steps in zip(sources, plan):
            share = (source.shape[0], source.shape[1] // team)
            shapes += [jax.ShapeDtypeStruct(share, source.dtype)] * steps
        pieces = list(
            pl.pallas_call(
                functools.partial(deal_kernel, team, depth, plan),
                out_shape=shapes,
                in_specs=[pl.BlockSpec(memory_space=pltpu.SMEM)]
                + [pl.BlockSpec(memory_space=pltpu.HBM)] * len(sources),
                out_specs=[pl.BlockSpec(memory_space=pltpu.VMEM)] * len(shapes),
                scratch_shapes=[pltpu.VMEM(source.shape, source.dtype) for source in sources]
                + [pltpu.SemaphoreType.DMA((CHUNKS * len(sources),))],
                compiler_params=pltpu.CompilerParams(vmem_limit_bytes=VMEM_LIMIT),
            )(info, *sources)
        )
    else:
        for source, steps in zip(sources, plan):
            rows, width = source.shape
            cut = source.reshape(rows, width // (team * depth), team, depth)
            for step in range(steps):
                share = lax.dynamic_index_in_dim(cut, info[0] ^ step, 2, keepdims=False)
                pieces.append(share.reshape(rows, -1))
    return [[pieces.pop(0) for _ in range(steps)] for steps in plan]


def spread(values, me, lanes, wide, above):
    per = values[0].shape[0] // BLOCK
    for step in range(TEAM):
        for b in range(per):
            rows = values[step][b * BLOCK : (b + 1) * BLOCK, lanes].astype(f32)
            wide[(me ^ step) * per + b, above:, :] = rows


def tile_lanes(info_ref, slot):
    return pl.ds(pl.multiple_of(info_ref[3 + slot] * LANES, LANES), LANES)


def state_kernel(info_ref, *refs):
    values = refs[:TEAM]
    rate_ref, starts_ref, end_ref, wide = refs[TEAM:]
    order = rate_ref.shape[0]
    me = info_ref[0]

    @pl.loop(0, starts_ref.shape[0])
    def _(slot):
        lanes = tile_lanes(info_ref, slot)
        spread(values, me, lanes, wide, 0)
        rate = rate_ref[:, lanes]
        lam, lam8 = jnp.exp(-rate), jnp.exp(-8.0 * rate)

        def block(b, state):
            starts_ref[slot, b] = state
            for at in range(0, BLOCK, 8):
                inflow = jnp.broadcast_to(wide[b, at : at + 1, :], (order, LANES))
                for t in range(1, 8):
                    inflow = lam * inflow + wide[b, at + t : at + t + 1, :]
                state = lam8 * state + inflow
            return state

        zero = jnp.zeros((order, LANES), f32)
        end_ref[:, lanes] = lax.fori_loop(0, wide.shape[0], block, zero, unroll=4)


def taps_kernel(base, info_ref, *refs):
    values = refs[:TEAM]
    rate_ref, coef_ref, skip_ref, y_ref, wide, taps = refs[TEAM:]
    me = info_ref[0]
    wide[:, :BLOCK, :] = jnp.zeros((wide.shape[0], BLOCK, LANES), f32)

    @pl.loop(0, y_ref.shape[0])
    def _(slot):
        lanes = tile_lanes(info_ref, base + slot)
        spread(values, me, lanes, wide, BLOCK)
        skip = skip_ref[:, lanes]
        lam = jnp.exp(-rate_ref[:, lanes])
        power = coef_ref[:, lanes]
        for t in range(BLOCK):
            tap = jnp.sum(power, axis=0, keepdims=True).astype(bf16).astype(f32)
            taps[t] = jnp.broadcast_to(tap, (8, LANES))
            power = power * lam

        @pl.loop(0, wide.shape[0])
        def _(b):
            y = [skip * wide[b, BLOCK + 8 * i : BLOCK + 8 * i + 8, :] for i in range(BLOCK // 8)]
            for t in range(BLOCK):
                tap = taps[t]
                for i in range(t // 8, BLOCK // 8):
                    at = BLOCK + 8 * i - t
                    y[i] = y[i] + tap * wide[b, at : at + 8, :]
            for i in range(BLOCK // 8):
                y_ref[slot, pl.ds(pl.multiple_of(b * BLOCK + 8 * i, 8), 8), :] = y[i]


def pair_kernel(span, info_ref, end_ref, near_ref, rate_ref, out_ref):
    high = info_ref[1] == 1
    first = jnp.where(high, near_ref[...], end_ref[...])
    second = jnp.where(high, end_ref[...], near_ref[...])
    out_ref[...] = jnp.exp(-span * rate_ref[...]) * first + second


def gate_kernel(base, reaches, info_ref, *refs):
    gaps = len(reaches)
    gates = refs[:TEAM]
    y_ref, starts_ref, rate_ref, coef_ref, near_ref = refs[TEAM : TEAM + 5]
    far = refs[TEAM + 5 : TEAM + 5 + gaps]
    out_ref, reach, decay8, start = refs[TEAM + 5 + gaps :]
    me, high = info_ref[0], info_ref[1]
    order = rate_ref.shape[0]
    rows = gates[0].shape[0]
    per = rows // BLOCK
    span = float(TEAM * rows)
    ahead = lax.broadcasted_iota(jnp.int32, (8, LANES), 0).astype(f32) + 1.0

    @pl.loop(0, y_ref.shape[0])
    def _(slot):
        lanes = tile_lanes(info_ref, base + slot)
        rate, coef = rate_ref[:, lanes], coef_ref[:, lanes]
        for k in range(order):
            reach[k] = coef[k : k + 1] * jnp.exp(-ahead * rate[k : k + 1])
            decay8[k] = jnp.exp(jnp.broadcast_to(-8.0 * rate[k : k + 1], (8, LANES)))
        state = jnp.zeros((order, LANES), f32)
        for gap, ref in zip(reaches, far):
            state = state + jnp.exp(-2.0 * span * gap * rate) * ref[:, lanes]
        after = jnp.exp(-span * rate) * state + near_ref[:, lanes]
        state = jnp.where(high == 1, after, state)
        over = jnp.exp(-float(BLOCK) * rate)
        for step in range(TEAM):
            place = me ^ step
            goes = place ^ (me & 2)
            entering = state * jnp.exp(-(rows * place).astype(f32) * rate)
            for b in range(per):
                start[b] = starts_ref[base + slot, place * per + b] + entering
                entering = entering * over
            for b in range(per):
                y = []
                for i in range(BLOCK // 8):
                    here = pl.multiple_of(place * rows + b * BLOCK + 8 * i, 8)
                    y.append(y_ref[slot, pl.ds(here, 8), :])
                for k in range(order):
                    term = reach[k] * start[b, k : k + 1, :]
                    decay = decay8[k]
                    for i in range(BLOCK // 8):
                        y[i] = y[i] + term
                        if i + 1 < BLOCK // 8:
                            term = term * decay
                for i in range(0, BLOCK // 8, 2):
                    at = b * BLOCK + 8 * i
                    conv = jnp.concatenate(y[i : i + 2], axis=0)
                    gated = gates[step][at : at + 16, lanes].astype(f32) * conv
                    to = pl.ds(pl.multiple_of(goes * rows + at, 16), 16)
                    out_ref[slot, to, :] = gated.astype(bf16)


def product(pieces, in_slots, first, info_ref, gated, weights, into, before):
    per = gated[0].shape[0]
    wide = into.shape[1]
    step = min(wide, 256)
    for slot in range(0, len(weights), 2):
        if in_slots:
            left = [gated[n // per][n % per] for n in (first + slot, first + slot + 1)]
        else:
            left = [gated[0][info_ref[3 + n]] for n in (first + slot, first + slot + 1)]
        left = jnp.concatenate(left, axis=1)
        for col in range(0, wide, step):
            right = jnp.concatenate([ref[:, col : col + step] for ref in weights[slot : slot + 2]], axis=0)
            term = jnp.dot(left, right, preferred_element_type=f32)
            cols = slice(col, col + step)
            start = before if slot == 0 else into
            into[:, cols] = term if start is None else start[:, cols] + term


def early_kernel(pieces, in_slots, info_ref, *refs):
    product(pieces, in_slots, 0, info_ref, refs[:pieces], refs[pieces:-1], refs[-1], None)


def project_kernel(pieces, in_slots, slots, at, info_ref, *refs):
    gated, (early_ref, near_ref, away_ref) = refs[:pieces], refs[pieces : pieces + 3]
    kept_ref, sent_ref, total = refs[-3:]
    core = info_ref[2]
    rows, wide = kept_ref.shape[0] // 2, kept_ref.shape[1]
    cols = slice(at, at + wide)
    weights = [near_ref.at[:, cols], away_ref]
    product(pieces, in_slots, slots - 2, info_ref, gated, weights, total, early_ref.at[:, cols])
    for across in range(2):
        here = slice(across * rows, (across + 1) * rows)
        for which, out in enumerate((kept_ref, sent_ref)):
            start = (2 * across + (core ^ which)) * rows
            out[here, :] = total[pl.ds(pl.multiple_of(start, rows), rows), :].astype(out.dtype)


def join_kernel(info_ref, kept_ref, got_ref, mine_ref, away_ref):
    rows = mine_ref.shape[0]
    mine_ref[...] = kept_ref[:rows, :] + got_ref[:rows, :].astype(f32)
    away_ref[...] = (kept_ref[rows:, :] + got_ref[rows:, :].astype(f32)).astype(bf16)


def finish_kernel(info_ref, *refs):
    out_ref = refs[-1]
    at = 0
    for mine, far in zip(refs[:-1:2], refs[1:-1:2]):
        wide = mine.shape[1]
        out_ref[:, at : at + wide] = (mine[...] + far[...].astype(f32)).astype(bf16)
        at += wide


def on_device(q_gate, values_in, decay_rate, residue, skip_gain, out_weight):
    rows, width = q_gate.shape
    depth, features = out_weight.shape
    order = decay_rate.shape[1]
    count = lax.axis_size("seq")
    heights = count // (2 * TEAM)
    mine = lax.axis_index("seq")
    me, core = mine % TEAM, mine % 2
    y, z = (mine // TEAM) % 2, mine // (2 * TEAM)
    share = width // TEAM

    def swap(value, bit):
        return lax.ppermute(value, "seq", [(i, i ^ bit) for i in range(count)])

    def up(value, gap, wrap):
        hop = gap * 2 * TEAM
        pairs = [(i, (i + hop) % count) for i in range(count) if wrap or i + hop < count]
        return lax.ppermute(value, "seq", pairs)

    in_slots = depth % LANES == 0
    groups = []
    for gap in range(heights):
        at = (z - gap) % heights
        groups += [at * 2 + y, at * 2 + (1 - y)]
    tiles = share // LANES
    order_of = groups if in_slots else list(range(tiles))
    info = jnp.stack([jnp.int32(n) for n in [me, y, core] + order_of])
    group_info = info if in_slots else jnp.stack([jnp.int32(n) for n in [me, y, core] + groups])

    def share_out(shares):
        return [shares[0]] + [swap(shares[step], step) for step in range(1, TEAM)]

    def share_out(shares):
        return [shares[0]] + [swap(shares[step], step) for step in range(1, TEAM)]

    def next_round(block):
        return up(block, 1, True), swap(block, TEAM)

    last = heights - 1
    weights, weights_away = [out_weight], []
    if last > 0:
        above, away = next_round(out_weight)
        weights.append(above)
        weights_away.append(away)

    (values,) = deal(info, TEAM, depth, [values_in], [TEAM])
    values = share_out(values)
    gates, rates, residues, skip = deal(
        info, TEAM, depth, [q_gate, decay_rate.T, residue.T, skip_gain[None]], [TEAM, 1, 1, 1]
    )
    rates, residues, skip = rates[0], residues[0], skip[0]
    coef = residues * jnp.sqrt(-jnp.expm1(-2.0 * rates))
    gates = share_out(gates[:2] + [tied(gate, values[3]) for gate in gates[2:]])

    blocks = TEAM * rows // BLOCK
    starts, end = call(
        state_kernel,
        [
            jax.ShapeDtypeStruct((tiles, blocks, order, LANES), f32),
            jax.ShapeDtypeStruct((order, share), f32),
        ],
        [pltpu.VMEM((blocks, BLOCK, LANES), f32)],
        after=[weights[-1], weights_away[-1]],
        micros=0.5,
    )(info, *values, rates)

    pieces = 4
    some = tiles // pieces
    if len(weights) < heights:
        above, away = next_round(tied(weights[-1], weights_away[-1], rates, values[1]))
        weights.append(above)
        weights_away.append(away)
    local = []
    for part in range(pieces):
        local.append(
            call(
                functools.partial(taps_kernel, part * some),
                jax.ShapeDtypeStruct((some, TEAM * rows, LANES), f32),
                [pltpu.VMEM((blocks, 2 * BLOCK, LANES), f32), pltpu.VMEM((BLOCK, 8, LANES), f32)],
                after=[end] if part == 0 else [local[-1]] + ([weights[-1], weights_away[-1]] if part > 1 else []),
                micros=0.3,
            )(info, *values, rates, coef, skip)
        )

    near = swap(end, TEAM)
    end = tied(end, local[0], local[1], *gates)
    span = float(TEAM * rows)
    held = call(
        functools.partial(pair_kernel, span), jax.ShapeDtypeStruct((order, share), f32), micros=0.2
    )(info, end, near, rates)
    while len(weights) < heights:
        above, away = next_round(tied(weights[-1], weights_away[-1], near, local[1], *gates))
        weights.append(above)
        weights_away.append(away)
    far, gap = [], 1
    while gap < heights:
        lags = [n * gap for n in (1, 2, 3) if n * gap < heights]
        far += [(lag - 1, up(held, lag, False)) for lag in lags]
        for lag, (_, state) in zip(lags, far[-len(lags) :]):
            held = held + jnp.exp(-2.0 * span * lag * rates) * state
        gap *= 4
    wide = features // LAST_PARTS
    block = tied(weights[last], weights_away[-1], local[-1])
    finals = [swap(block[:, part * wide : (part + 1) * wide], TEAM) for part in range(LAST_PARTS)]

    tables = [pltpu.VMEM((order, 8, LANES), f32)] * 2
    gated = [
        call(
            functools.partial(gate_kernel, part * some, [lag for lag, _ in far]),
            jax.ShapeDtypeStruct((some, TEAM * rows, LANES), bf16),
            tables + [pltpu.VMEM((rows // BLOCK, order, LANES), f32)],
            after=[local[-1]] if part < 2 else [weights[last], weights_away[-1]],
            micros=0.5,
        )(info, *gates, local[part], starts, rates, coef, near, *[state for _, state in far])
        for part in range(pieces)
    ]
    if not in_slots:
        gated = jnp.concatenate(gated, axis=0).transpose(1, 0, 2)
        gated = gated.reshape(TEAM * rows, width // (TEAM * depth), depth).transpose(1, 0, 2)
        gated = [gated]

    early = call(
        functools.partial(early_kernel, len(gated), in_slots),
        jax.ShapeDtypeStruct((TEAM * rows, features), f32),
        micros=1.0,
    )(group_info, *gated, *[ref for pair in zip(weights, weights_away) for ref in pair])
    finished, joined = [], []
    for part, final in enumerate(finals):
        kept, sent = call(
            functools.partial(project_kernel, len(gated), in_slots, 2 * heights, part * wide),
            [jax.ShapeDtypeStruct((2 * rows, wide), dtype) for dtype in (f32, bf16)],
            [pltpu.VMEM((TEAM * rows, wide), f32)],
            micros=0.3,
        )(group_info, *gated, early, weights[last], final)
        mine_sum, away_sum = call(
            join_kernel,
            [jax.ShapeDtypeStruct((rows, wide), f32), jax.ShapeDtypeStruct((rows, wide), bf16)],
        )(info, kept, swap(sent, 1))
        joined.append(mine_sum)
        finished += [mine_sum, swap(away_sum, 2)]
    return call(finish_kernel, jax.ShapeDtypeStruct((rows, features), bf16))(info, *finished)


def solution(mesh):
    in_specs = (
        P(("groups", "seq"), None),
        P(("groups", "seq"), None),
        P(),
        P(),
        P(),
        P("seq", None),
    )
    out_specs = P(("groups", "seq"), None)
    return jax.shard_map(
        on_device, mesh=mesh, in_specs=in_specs, out_specs=out_specs, check_vma=False
    )
```

```python
import functools

import jax
import jax.numpy as jnp
from jax import lax
from jax.experimental import pallas as pl
from jax.experimental.pallas import tpu as pltpu
from jax.sharding import PartitionSpec as P

BLOCK = 32
LANES = 128
CHUNKS = 8
TEAM = 4
VMEM_LIMIT = 8 * 1024 * 1024

f32 = jnp.float32
bf16 = jnp.bfloat16


def tied(value, *others):
    return lax.optimization_barrier((value, *others))[0]


def call(kernel, out_shape, scratch=(), after=(), micros=0.0):
    def run(info, *args):
        return pl.pallas_call(
            kernel,
            out_shape=out_shape,
            in_specs=[pl.BlockSpec(memory_space=pltpu.SMEM)] + [pl.BlockSpec()] * len(args),
            scratch_shapes=list(scratch),
            compiler_params=pltpu.CompilerParams(vmem_limit_bytes=VMEM_LIMIT),
            cost_estimate=pl.CostEstimate(
                flops=int(micros * 1.1e9), bytes_accessed=int(micros * 3.6e6), transcendentals=0
            ),
        )(tied(info, *after), *args)

    return run


def deal_kernel(team, depth, plan, info_ref, *refs):
    me = info_ref[0]
    count = len(plan)
    sources, held, sems = refs[:count], refs[-1 - count : -1], refs[-1]
    outs = list(refs[count : -1 - count])
    copies = []
    for source, whole in zip(sources, held):
        wide = source.shape[1] // CHUNKS
        for chunk in range(CHUNKS):
            cols = slice(chunk * wide, (chunk + 1) * wide)
            sem = sems.at[len(copies)]
            copies.append(pltpu.make_async_copy(source.at[:, cols], whole.at[:, cols], sem))
            copies[-1].start()
    for source, whole, steps in zip(sources, held, plan):
        runs = source.shape[1] // (team * depth)
        mine = [outs.pop(0) for _ in range(steps)]
        for run in range(runs):
            if run % (runs // CHUNKS) == 0:
                copies.pop(0).wait()
            for step in range(steps):
                at = pl.multiple_of((run * team + (me ^ step)) * depth, depth)
                mine[step][:, run * depth : (run + 1) * depth] = whole[:, pl.ds(at, depth)]


def deal(info, team, depth, sources, plan):
    pieces = []
    if depth % LANES == 0:
        shapes = []
        for source, steps in zip(sources, plan):
            share = (source.shape[0], source.shape[1] // team)
            shapes += [jax.ShapeDtypeStruct(share, source.dtype)] * steps
        pieces = list(
            pl.pallas_call(
                functools.partial(deal_kernel, team, depth, plan),
                out_shape=shapes,
                in_specs=[pl.BlockSpec(memory_space=pltpu.SMEM)]
                + [pl.BlockSpec(memory_space=pltpu.HBM)] * len(sources),
                out_specs=[pl.BlockSpec(memory_space=pltpu.VMEM)] * len(shapes),
                scratch_shapes=[pltpu.VMEM(source.shape, source.dtype) for source in sources]
                + [pltpu.SemaphoreType.DMA((CHUNKS * len(sources),))],
                compiler_params=pltpu.CompilerParams(vmem_limit_bytes=VMEM_LIMIT),
            )(info, *sources)
        )
    else:
        for source, steps in zip(sources, plan):
            rows, width = source.shape
            cut = source.reshape(rows, width // (team * depth), team, depth)
            for step in range(steps):
                share = lax.dynamic_index_in_dim(cut, info[0] ^ step, 2, keepdims=False)
                pieces.append(share.reshape(rows, -1))
    return [[pieces.pop(0) for _ in range(steps)] for steps in plan]


def spread(values, me, lanes, wide, above):
    per = values[0].shape[0] // BLOCK
    for step in range(TEAM):
        for b in range(per):
            rows = values[step][b * BLOCK : (b + 1) * BLOCK, lanes].astype(f32)
            wide[(me ^ step) * per + b, above:, :] = rows


def tile_lanes(info_ref, slot):
    return pl.ds(pl.multiple_of(info_ref[3 + slot] * LANES, LANES), LANES)


def state_kernel(info_ref, *refs):
    values = refs[:TEAM]
    rate_ref, starts_ref, end_ref, wide = refs[TEAM:]
    order = rate_ref.shape[0]
    me = info_ref[0]

    @pl.loop(0, starts_ref.shape[0])
    def _(slot):
        lanes = tile_lanes(info_ref, slot)
        spread(values, me, lanes, wide, 0)
        rate = rate_ref[:, lanes]
        lam, lam8 = jnp.exp(-rate), jnp.exp(-8.0 * rate)

        def block(b, state):
            starts_ref[slot, b] = state
            for at in range(0, BLOCK, 8):
                inflow = jnp.broadcast_to(wide[b, at : at + 1, :], (order, LANES))
                for t in range(1, 8):
                    inflow = lam * inflow + wide[b, at + t : at + t + 1, :]
                state = lam8 * state + inflow
            return state

        zero = jnp.zeros((order, LANES), f32)
        end_ref[:, lanes] = lax.fori_loop(0, wide.shape[0], block, zero, unroll=4)


def taps_kernel(base, info_ref, *refs):
    values = refs[:TEAM]
    rate_ref, coef_ref, skip_ref, y_ref, wide, taps = refs[TEAM:]
    me = info_ref[0]
    wide[:, :BLOCK, :] = jnp.zeros((wide.shape[0], BLOCK, LANES), f32)

    @pl.loop(0, y_ref.shape[0])
    def _(slot):
        lanes = tile_lanes(info_ref, base + slot)
        spread(values, me, lanes, wide, BLOCK)
        skip = skip_ref[:, lanes]
        lam = jnp.exp(-rate_ref[:, lanes])
        power = coef_ref[:, lanes]
        for t in range(BLOCK):
            tap = jnp.sum(power, axis=0, keepdims=True).astype(bf16).astype(f32)
            taps[t] = jnp.broadcast_to(tap, (8, LANES))
            power = power * lam

        @pl.loop(0, wide.shape[0])
        def _(b):
            y = [skip * wide[b, BLOCK + 8 * i : BLOCK + 8 * i + 8, :] for i in range(BLOCK // 8)]
            for t in range(BLOCK):
                tap = taps[t]
                for i in range(t // 8, BLOCK // 8):
                    at = BLOCK + 8 * i - t
                    y[i] = y[i] + tap * wide[b, at : at + 8, :]
            for i in range(BLOCK // 8):
                y_ref[slot, pl.ds(pl.multiple_of(b * BLOCK + 8 * i, 8), 8), :] = y[i]


def pair_kernel(span, info_ref, end_ref, near_ref, rate_ref, out_ref):
    high = info_ref[1] == 1
    first = jnp.where(high, near_ref[...], end_ref[...])
    second = jnp.where(high, end_ref[...], near_ref[...])
    out_ref[...] = jnp.exp(-span * rate_ref[...]) * first + second


def gate_kernel(base, reaches, info_ref, *refs):
    gaps = len(reaches)
    gates = refs[:TEAM]
    y_ref, starts_ref, rate_ref, coef_ref, near_ref = refs[TEAM : TEAM + 5]
    far = refs[TEAM + 5 : TEAM + 5 + gaps]
    out_ref, reach, decay8, start = refs[TEAM + 5 + gaps :]
    me, high = info_ref[0], info_ref[1]
    order = rate_ref.shape[0]
    rows = gates[0].shape[0]
    per = rows // BLOCK
    span = float(TEAM * rows)
    ahead = lax.broadcasted_iota(jnp.int32, (8, LANES), 0).astype(f32) + 1.0

    @pl.loop(0, y_ref.shape[0])
    def _(slot):
        lanes = tile_lanes(info_ref, base + slot)
        rate, coef = rate_ref[:, lanes], coef_ref[:, lanes]
        for k in range(order):
            reach[k] = coef[k : k + 1] * jnp.exp(-ahead * rate[k : k + 1])
            decay8[k] = jnp.exp(jnp.broadcast_to(-8.0 * rate[k : k + 1], (8, LANES)))
        state = jnp.zeros((order, LANES), f32)
        for gap, ref in zip(reaches, far):
            state = state + jnp.exp(-2.0 * span * gap * rate) * ref[:, lanes]
        after = jnp.exp(-span * rate) * state + near_ref[:, lanes]
        state = jnp.where(high == 1, after, state)
        over = jnp.exp(-float(BLOCK) * rate)
        for step in range(TEAM):
            place = me ^ step
            goes = place ^ (me & 2)
            entering = state * jnp.exp(-(rows * place).astype(f32) * rate)
            for b in range(per):
                start[b] = starts_ref[base + slot, place * per + b] + entering
                entering = entering * over
            for b in range(per):
                y = []
                for i in range(BLOCK // 8):
                    here = pl.multiple_of(place * rows + b * BLOCK + 8 * i, 8)
                    y.append(y_ref[slot, pl.ds(here, 8), :])
                for k in range(order):
                    term = reach[k] * start[b, k : k + 1, :]
                    decay = decay8[k]
                    for i in range(BLOCK // 8):
                        y[i] = y[i] + term
                        if i + 1 < BLOCK // 8:
                            term = term * decay
                for i in range(0, BLOCK // 8, 2):
                    at = b * BLOCK + 8 * i
                    conv = jnp.concatenate(y[i : i + 2], axis=0)
                    gated = gates[step][at : at + 16, lanes].astype(f32) * conv
                    to = pl.ds(pl.multiple_of(goes * rows + at, 16), 16)
                    out_ref[slot, to, :] = gated.astype(bf16)


def product(pieces, in_slots, first, info_ref, gated, weights, into, before):
    per = gated[0].shape[0]
    wide = into.shape[1]
    step = min(wide, 256)
    slots = range(first, first + len(weights))
    if in_slots:
        left = [gated[slot // per][slot % per] for slot in slots]
    else:
        left = [gated[0][info_ref[3 + slot]] for slot in slots]
    left = jnp.concatenate(left, axis=1)
    for col in range(0, wide, step):
        cols = slice(col, col + step)
        right = jnp.concatenate([ref[:, cols] for ref in weights], axis=0)
        total = jnp.dot(left, right, preferred_element_type=f32)
        into[:, cols] = total if before is None else before[:, cols] + total


def project_kernel(pieces, in_slots, at, info_ref, *refs):
    gated, weights = refs[:pieces], refs[pieces:-3]
    kept_ref, sent_ref, total = refs[-3:]
    core = info_ref[2]
    rows, wide = kept_ref.shape[0] // 2, kept_ref.shape[1]
    weights = [ref.at[:, at : at + wide] for ref in weights[:-1]] + [weights[-1]]
    product(pieces, in_slots, 0, info_ref, gated, weights, total, None)
    for across in range(2):
        here = slice(across * rows, (across + 1) * rows)
        for which, out in enumerate((kept_ref, sent_ref)):
            start = (2 * across + (core ^ which)) * rows
            out[here, :] = total[pl.ds(pl.multiple_of(start, rows), rows), :].astype(out.dtype)


def join_kernel(info_ref, kept_ref, got_ref, mine_ref, away_ref):
    rows = mine_ref.shape[0]
    mine_ref[...] = kept_ref[:rows, :] + got_ref[:rows, :].astype(f32)
    away_ref[...] = (kept_ref[rows:, :] + got_ref[rows:, :].astype(f32)).astype(bf16)


def finish_kernel(info_ref, *refs):
    out_ref = refs[-1]
    at = 0
    for mine, far in zip(refs[:-1:2], refs[1:-1:2]):
        wide = mine.shape[1]
        out_ref[:, at : at + wide] = (mine[...] + far[...].astype(f32)).astype(bf16)
        at += wide


def on_device(q_gate, values_in, decay_rate, residue, skip_gain, out_weight):
    rows, width = q_gate.shape
    depth, features = out_weight.shape
    order = decay_rate.shape[1]
    count = lax.axis_size("seq")
    heights = count // (2 * TEAM)
    mine = lax.axis_index("seq")
    me, core = mine % TEAM, mine % 2
    y, z = (mine // TEAM) % 2, mine // (2 * TEAM)
    share = width // TEAM

    def swap(value, bit):
        return lax.ppermute(value, "seq", [(i, i ^ bit) for i in range(count)])

    def up(value, gap, wrap):
        hop = gap * 2 * TEAM
        pairs = [(i, (i + hop) % count) for i in range(count) if wrap or i + hop < count]
        return lax.ppermute(value, "seq", pairs)

    in_slots = depth % LANES == 0
    groups = []
    for gap in range(heights):
        at = (z - gap) % heights
        groups += [at * 2 + y, at * 2 + (1 - y)]
    tiles = share // LANES
    order_of = groups if in_slots else list(range(tiles))
    info = jnp.stack([jnp.int32(n) for n in [me, y, core] + order_of])
    group_info = info if in_slots else jnp.stack([jnp.int32(n) for n in [me, y, core] + groups])

    def share_out(shares):
        return [shares[0]] + [swap(shares[step], step) for step in range(1, TEAM)]

    def next_round(block):
        return up(block, 1, True), swap(block, TEAM)

    last = heights - 1
    weights, weights_away = [out_weight], []
    if last > 0:
        above, away = next_round(out_weight)
        weights.append(above)
        weights_away.append(away)

    (values,) = deal(info, TEAM, depth, [values_in], [TEAM])
    values = share_out(values)
    gates, rates, residues, skip = deal(
        info, TEAM, depth, [q_gate, decay_rate.T, residue.T, skip_gain[None]], [TEAM, 1, 1, 1]
    )
    rates, residues, skip = rates[0], residues[0], skip[0]
    coef = residues * jnp.sqrt(-jnp.expm1(-2.0 * rates))
    gates = share_out(gates[:2] + [tied(gate, values[3]) for gate in gates[2:]])

    blocks = TEAM * rows // BLOCK
    starts, end = call(
        state_kernel,
        [
            jax.ShapeDtypeStruct((tiles, blocks, order, LANES), f32),
            jax.ShapeDtypeStruct((order, share), f32),
        ],
        [pltpu.VMEM((blocks, BLOCK, LANES), f32)],
        after=[weights[-1], weights_away[-1]],
        micros=0.5,
    )(info, *values, rates)

    pieces = 4
    some = tiles // pieces
    if len(weights) < heights:
        above, away = next_round(tied(weights[-1], weights_away[-1], rates, values[1]))
        weights.append(above)
        weights_away.append(away)
    local = []
    for part in range(pieces):
        local.append(
            call(
                functools.partial(taps_kernel, part * some),
                jax.ShapeDtypeStruct((some, TEAM * rows, LANES), f32),
                [pltpu.VMEM((blocks, 2 * BLOCK, LANES), f32), pltpu.VMEM((BLOCK, 8, LANES), f32)],
                after=[end] if part == 0 else [local[-1]] + ([weights[-1], weights_away[-1]] if part > 1 else []),
                micros=0.3,
            )(info, *values, rates, coef, skip)
        )

    near = swap(end, TEAM)
    end = tied(end, local[0], local[1], *gates)
    span = float(TEAM * rows)
    held = call(
        functools.partial(pair_kernel, span), jax.ShapeDtypeStruct((order, share), f32), micros=0.2
    )(info, end, near, rates)
    while len(weights) < heights:
        above, away = next_round(tied(weights[-1], weights_away[-1], near, local[1], *gates))
        weights.append(above)
        weights_away.append(away)
    far, gap = [], 1
    while gap < heights:
        lags = [n * gap for n in (1, 2, 3) if n * gap < heights]
        far += [(lag - 1, up(held, lag, False)) for lag in lags]
        for lag, (_, state) in zip(lags, far[-len(lags) :]):
            held = held + jnp.exp(-2.0 * span * lag * rates) * state
        gap *= 4
    wide = features // 2
    mine, theirs = lax.optimization_barrier((weights[last], weights_away[-1], local[-1]))[:2]
    finals = [swap(mine[:, :wide], TEAM), up(theirs[:, wide:], 1, True)]

    tables = [pltpu.VMEM((order, 8, LANES), f32)] * 2
    gated = [
        call(
            functools.partial(gate_kernel, part * some, [lag for lag, _ in far]),
            jax.ShapeDtypeStruct((some, TEAM * rows, LANES), bf16),
            tables + [pltpu.VMEM((rows // BLOCK, order, LANES), f32)],
            after=[local[-1]] if part < 2 else [weights[last], weights_away[-1]],
            micros=0.5,
        )(info, *gates, local[part], starts, rates, coef, near, *[state for _, state in far])
        for part in range(pieces)
    ]
    if not in_slots:
        gated = jnp.concatenate(gated, axis=0).transpose(1, 0, 2)
        gated = gated.reshape(TEAM * rows, width // (TEAM * depth), depth).transpose(1, 0, 2)
        gated = [gated]

    slots = [ref for pair in zip(weights, weights_away) for ref in pair] + [weights[last]]
    finished, joined = [], []
    for part, final in enumerate(finals):
        kept, sent = call(
            functools.partial(project_kernel, len(gated), in_slots, part * wide),
            [jax.ShapeDtypeStruct((2 * rows, wide), dtype) for dtype in (f32, bf16)],
            [pltpu.VMEM((TEAM * rows, wide), f32)],
            micros=1.0,
        )(group_info, *gated, *slots, final)
        mine_sum, away_sum = call(
            join_kernel,
            [jax.ShapeDtypeStruct((rows, wide), f32), jax.ShapeDtypeStruct((rows, wide), bf16)],
        )(info, kept, swap(sent, 1))
        joined.append(mine_sum)
        finished += [mine_sum, swap(away_sum, 2)]
    return call(finish_kernel, jax.ShapeDtypeStruct((rows, features), bf16))(info, *finished)


def solution(mesh):
    in_specs = (
        P(("groups", "seq"), None),
        P(("groups", "seq"), None),
        P(),
        P(),
        P(),
        P("seq", None),
    )
    out_specs = P(("groups", "seq"), None)
    return jax.shard_map(
        on_device, mesh=mesh, in_specs=in_specs, out_specs=out_specs, check_vma=False
    )
```

```python
import functools

import jax
import jax.numpy as jnp
from jax import lax
from jax.experimental import pallas as pl
from jax.experimental.pallas import tpu as pltpu
from jax.sharding import PartitionSpec as P

BLOCK = 32
LANES = 128
CHUNKS = 8
TEAM = 4
VMEM_LIMIT = 8 * 1024 * 1024

f32 = jnp.float32
bf16 = jnp.bfloat16


def tied(value, *others):
    return lax.optimization_barrier((value, *others))[0]


def call(kernel, out_shape, scratch=(), after=(), micros=0.0):
    def run(info, *args):
        return pl.pallas_call(
            kernel,
            out_shape=out_shape,
            in_specs=[pl.BlockSpec(memory_space=pltpu.SMEM)] + [pl.BlockSpec()] * len(args),
            scratch_shapes=list(scratch),
            compiler_params=pltpu.CompilerParams(vmem_limit_bytes=VMEM_LIMIT),
            cost_estimate=pl.CostEstimate(
                flops=int(micros * 1.1e9), bytes_accessed=int(micros * 3.6e6), transcendentals=0
            ),
        )(tied(info, *after), *args)

    return run


def deal_kernel(team, depth, plan, info_ref, *refs):
    me = info_ref[0]
    count = len(plan)
    sources, held, sems = refs[:count], refs[-1 - count : -1], refs[-1]
    outs = list(refs[count : -1 - count])
    copies = []
    for source, whole in zip(sources, held):
        wide = source.shape[1] // CHUNKS
        for chunk in range(CHUNKS):
            cols = slice(chunk * wide, (chunk + 1) * wide)
            sem = sems.at[len(copies)]
            copies.append(pltpu.make_async_copy(source.at[:, cols], whole.at[:, cols], sem))
            copies[-1].start()
    for source, whole, steps in zip(sources, held, plan):
        runs = source.shape[1] // (team * depth)
        mine = [outs.pop(0) for _ in range(steps)]
        for run in range(runs):
            if run % (runs // CHUNKS) == 0:
                copies.pop(0).wait()
            for step in range(steps):
                at = pl.multiple_of((run * team + (me ^ step)) * depth, depth)
                mine[step][:, run * depth : (run + 1) * depth] = whole[:, pl.ds(at, depth)]


def deal(info, team, depth, sources, plan):
    pieces = []
    if depth % LANES == 0:
        shapes = []
        for source, steps in zip(sources, plan):
            share = (source.shape[0], source.shape[1] // team)
            shapes += [jax.ShapeDtypeStruct(share, source.dtype)] * steps
        pieces = list(
            pl.pallas_call(
                functools.partial(deal_kernel, team, depth, plan),
                out_shape=shapes,
                in_specs=[pl.BlockSpec(memory_space=pltpu.SMEM)]
                + [pl.BlockSpec(memory_space=pltpu.HBM)] * len(sources),
                out_specs=[pl.BlockSpec(memory_space=pltpu.VMEM)] * len(shapes),
                scratch_shapes=[pltpu.VMEM(source.shape, source.dtype) for source in sources]
                + [pltpu.SemaphoreType.DMA((CHUNKS * len(sources),))],
                compiler_params=pltpu.CompilerParams(vmem_limit_bytes=VMEM_LIMIT),
            )(info, *sources)
        )
    else:
        for source, steps in zip(sources, plan):
            rows, width = source.shape
            cut = source.reshape(rows, width // (team * depth), team, depth)
            for step in range(steps):
                share = lax.dynamic_index_in_dim(cut, info[0] ^ step, 2, keepdims=False)
                pieces.append(share.reshape(rows, -1))
    return [[pieces.pop(0) for _ in range(steps)] for steps in plan]


def spread(values, me, lanes, wide, above):
    per = values[0].shape[0] // BLOCK
    for step in range(TEAM):
        for b in range(per):
            rows = values[step][b * BLOCK : (b + 1) * BLOCK, lanes].astype(f32)
            wide[(me ^ step) * per + b, above:, :] = rows


def tile_lanes(info_ref, slot):
    return pl.ds(pl.multiple_of(info_ref[3 + slot] * LANES, LANES), LANES)


def state_kernel(info_ref, *refs):
    values = refs[:TEAM]
    rate_ref, starts_ref, end_ref, wide = refs[TEAM:]
    order = rate_ref.shape[0]
    me = info_ref[0]

    @pl.loop(0, starts_ref.shape[0])
    def _(slot):
        lanes = tile_lanes(info_ref, slot)
        spread(values, me, lanes, wide, 0)
        rate = rate_ref[:, lanes]
        lam, lam8 = jnp.exp(-rate), jnp.exp(-8.0 * rate)

        def block(b, state):
            starts_ref[slot, b] = state
            for at in range(0, BLOCK, 8):
                inflow = jnp.broadcast_to(wide[b, at : at + 1, :], (order, LANES))
                for t in range(1, 8):
                    inflow = lam * inflow + wide[b, at + t : at + t + 1, :]
                state = lam8 * state + inflow
            return state

        zero = jnp.zeros((order, LANES), f32)
        end_ref[:, lanes] = lax.fori_loop(0, wide.shape[0], block, zero, unroll=4)


def taps_kernel(base, info_ref, *refs):
    values = refs[:TEAM]
    rate_ref, coef_ref, skip_ref, y_ref, wide, taps = refs[TEAM:]
    me = info_ref[0]
    wide[:, :BLOCK, :] = jnp.zeros((wide.shape[0], BLOCK, LANES), f32)

    @pl.loop(0, y_ref.shape[0])
    def _(slot):
        lanes = tile_lanes(info_ref, base + slot)
        spread(values, me, lanes, wide, BLOCK)
        skip = skip_ref[:, lanes]
        lam = jnp.exp(-rate_ref[:, lanes])
        power = coef_ref[:, lanes]
        for t in range(BLOCK):
            tap = jnp.sum(power, axis=0, keepdims=True).astype(bf16).astype(f32)
            taps[t] = jnp.broadcast_to(tap, (8, LANES))
            power = power * lam

        @pl.loop(0, wide.shape[0])
        def _(b):
            y = [skip * wide[b, BLOCK + 8 * i : BLOCK + 8 * i + 8, :] for i in range(BLOCK // 8)]
            for t in range(BLOCK):
                tap = taps[t]
                for i in range(t // 8, BLOCK // 8):
                    at = BLOCK + 8 * i - t
                    y[i] = y[i] + tap * wide[b, at : at + 8, :]
            for i in range(BLOCK // 8):
                y_ref[slot, pl.ds(pl.multiple_of(b * BLOCK + 8 * i, 8), 8), :] = y[i]


def pair_kernel(span, info_ref, end_ref, near_ref, rate_ref, out_ref):
    high = info_ref[1] == 1
    first = jnp.where(high, near_ref[...], end_ref[...])
    second = jnp.where(high, end_ref[...], near_ref[...])
    out_ref[...] = jnp.exp(-span * rate_ref[...]) * first + second


def gate_kernel(base, reaches, info_ref, *refs):
    gaps = len(reaches)
    gates = refs[:TEAM]
    y_ref, starts_ref, rate_ref, coef_ref, near_ref = refs[TEAM : TEAM + 5]
    far = refs[TEAM + 5 : TEAM + 5 + gaps]
    out_ref, reach, decay8, start = refs[TEAM + 5 + gaps :]
    me, high = info_ref[0], info_ref[1]
    order = rate_ref.shape[0]
    rows = gates[0].shape[0]
    per = rows // BLOCK
    span = float(TEAM * rows)
    ahead = lax.broadcasted_iota(jnp.int32, (8, LANES), 0).astype(f32) + 1.0

    @pl.loop(0, y_ref.shape[0])
    def _(slot):
        lanes = tile_lanes(info_ref, base + slot)
        rate, coef = rate_ref[:, lanes], coef_ref[:, lanes]
        for k in range(order):
            reach[k] = coef[k : k + 1] * jnp.exp(-ahead * rate[k : k + 1])
            decay8[k] = jnp.exp(jnp.broadcast_to(-8.0 * rate[k : k + 1], (8, LANES)))
        state = jnp.zeros((order, LANES), f32)
        for gap, ref in zip(reaches, far):
            state = state + jnp.exp(-2.0 * span * gap * rate) * ref[:, lanes]
        after = jnp.exp(-span * rate) * state + near_ref[:, lanes]
        state = jnp.where(high == 1, after, state)
        over = jnp.exp(-float(BLOCK) * rate)
        for step in range(TEAM):
            place = me ^ step
            goes = place ^ (me & 2)
            entering = state * jnp.exp(-(rows * place).astype(f32) * rate)
            for b in range(per):
                start[b] = starts_ref[base + slot, place * per + b] + entering
                entering = entering * over
            for b in range(per):
                y = []
                for i in range(BLOCK // 8):
                    here = pl.multiple_of(place * rows + b * BLOCK + 8 * i, 8)
                    y.append(y_ref[slot, pl.ds(here, 8), :])
                for k in range(order):
                    term = reach[k] * start[b, k : k + 1, :]
                    decay = decay8[k]
                    for i in range(BLOCK // 8):
                        y[i] = y[i] + term
                        if i + 1 < BLOCK // 8:
                            term = term * decay
                for i in range(0, BLOCK // 8, 2):
                    at = b * BLOCK + 8 * i
                    conv = jnp.concatenate(y[i : i + 2], axis=0)
                    gated = gates[step][at : at + 16, lanes].astype(f32) * conv
                    to = pl.ds(pl.multiple_of(goes * rows + at, 16), 16)
                    out_ref[slot, to, :] = gated.astype(bf16)


def product(pieces, in_slots, first, info_ref, gated, weights, into, before):
    per = gated[0].shape[0]
    wide = into.shape[1]
    step = min(wide, 256)
    slots = range(first, first + len(weights))
    if in_slots:
        left = [gated[slot // per][slot % per] for slot in slots]
    else:
        left = [gated[0][info_ref[3 + slot]] for slot in slots]
    left = jnp.concatenate(left, axis=1)
    for col in range(0, wide, step):
        cols = slice(col, col + step)
        right = jnp.concatenate([ref[:, cols] for ref in weights], axis=0)
        total = jnp.dot(left, right, preferred_element_type=f32)
        into[:, cols] = total if before is None else before[:, cols] + total


def project_kernel(pieces, in_slots, at, info_ref, *refs):
    gated, weights = refs[:pieces], refs[pieces:-3]
    kept_ref, sent_ref, total = refs[-3:]
    core = info_ref[2]
    rows, wide = kept_ref.shape[0] // 2, kept_ref.shape[1]
    weights = [ref.at[:, at : at + wide] for ref in weights[:-1]] + [weights[-1]]
    product(pieces, in_slots, 0, info_ref, gated, weights, total, None)
    for across in range(2):
        here = slice(across * rows, (across + 1) * rows)
        for which, out in enumerate((kept_ref, sent_ref)):
            start = (2 * across + (core ^ which)) * rows
            out[here, :] = total[pl.ds(pl.multiple_of(start, rows), rows), :].astype(out.dtype)


def join_kernel(info_ref, kept_ref, got_ref, mine_ref, away_ref):
    rows = mine_ref.shape[0]
    mine_ref[...] = kept_ref[:rows, :] + got_ref[:rows, :].astype(f32)
    away_ref[...] = (kept_ref[rows:, :] + got_ref[rows:, :].astype(f32)).astype(bf16)


def finish_kernel(at, info_ref, mine_ref, far_ref, *refs):
    out_ref, rounded, sem = refs[-3:]
    rounded[...] = (mine_ref[...] + far_ref[...].astype(f32)).astype(bf16)
    copy = pltpu.make_async_copy(rounded, out_ref.at[:, at : at + rounded.shape[1]], sem)
    copy.start()
    copy.wait()


def finish(info, at, features, mine, far, before):
    anywhere = pl.BlockSpec(memory_space=pl.ANY)
    return pl.pallas_call(
        functools.partial(finish_kernel, at),
        out_shape=jax.ShapeDtypeStruct((mine.shape[0], features), bf16),
        in_specs=[pl.BlockSpec(memory_space=pltpu.SMEM)]
        + [pl.BlockSpec()] * 2
        + [anywhere] * len(before),
        out_specs=anywhere,
        input_output_aliases={3: 0} if before else {},
        scratch_shapes=[pltpu.VMEM(mine.shape, bf16), pltpu.SemaphoreType.DMA],
        compiler_params=pltpu.CompilerParams(vmem_limit_bytes=VMEM_LIMIT),
    )(info, mine, far, *before)


def on_device(q_gate, values_in, decay_rate, residue, skip_gain, out_weight):
    rows, width = q_gate.shape
    depth, features = out_weight.shape
    order = decay_rate.shape[1]
    count = lax.axis_size("seq")
    heights = count // (2 * TEAM)
    mine = lax.axis_index("seq")
    me, core = mine % TEAM, mine % 2
    y, z = (mine // TEAM) % 2, mine // (2 * TEAM)
    share = width // TEAM

    def swap(value, bit):
        return lax.ppermute(value, "seq", [(i, i ^ bit) for i in range(count)])

    def up(value, gap, wrap):
        hop = gap * 2 * TEAM
        pairs = [(i, (i + hop) % count) for i in range(count) if wrap or i + hop < count]
        return lax.ppermute(value, "seq", pairs)

    in_slots = depth % LANES == 0
    groups = []
    for gap in range(heights):
        at = (z - gap) % heights
        groups += [at * 2 + y, at * 2 + (1 - y)]
    tiles = share // LANES
    order_of = groups if in_slots else list(range(tiles))
    info = jnp.stack([jnp.int32(n) for n in [me, y, core] + order_of])
    group_info = info if in_slots else jnp.stack([jnp.int32(n) for n in [me, y, core] + groups])

    def share_out(shares):
        return [shares[0]] + [swap(shares[step], step) for step in range(1, TEAM)]

    def next_round(block):
        return up(block, 1, True), swap(block, TEAM)

    last = heights - 1
    weights, weights_away = [out_weight], []
    if last > 0:
        above, away = next_round(out_weight)
        weights.append(above)
        weights_away.append(away)

    (values,) = deal(info, TEAM, depth, [values_in], [TEAM])
    values = share_out(values)
    gates, rates, residues, skip = deal(
        info, TEAM, depth, [q_gate, decay_rate.T, residue.T, skip_gain[None]], [TEAM, 1, 1, 1]
    )
    rates, residues, skip = rates[0], residues[0], skip[0]
    coef = residues * jnp.sqrt(-jnp.expm1(-2.0 * rates))
    gates = share_out(gates[:2] + [tied(gate, values[3]) for gate in gates[2:]])

    blocks = TEAM * rows // BLOCK
    starts, end = call(
        state_kernel,
        [
            jax.ShapeDtypeStruct((tiles, blocks, order, LANES), f32),
            jax.ShapeDtypeStruct((order, share), f32),
        ],
        [pltpu.VMEM((blocks, BLOCK, LANES), f32)],
        after=[weights[-1], weights_away[-1]],
        micros=0.5,
    )(info, *values, rates)

    pieces = 4
    some = tiles // pieces
    if len(weights) < heights:
        above, away = next_round(tied(weights[-1], weights_away[-1], rates, values[1]))
        weights.append(above)
        weights_away.append(away)
    local = []
    for part in range(pieces):
        local.append(
            call(
                functools.partial(taps_kernel, part * some),
                jax.ShapeDtypeStruct((some, TEAM * rows, LANES), f32),
                [pltpu.VMEM((blocks, 2 * BLOCK, LANES), f32), pltpu.VMEM((BLOCK, 8, LANES), f32)],
                after=[end] if part == 0 else [local[-1]] + ([weights[-1], weights_away[-1]] if part > 1 else []),
                micros=0.3,
            )(info, *values, rates, coef, skip)
        )

    near = swap(end, TEAM)
    end = tied(end, local[0], local[1], *gates)
    span = float(TEAM * rows)
    held = call(
        functools.partial(pair_kernel, span), jax.ShapeDtypeStruct((order, share), f32), micros=0.2
    )(info, end, near, rates)
    while len(weights) < heights:
        above, away = next_round(tied(weights[-1], weights_away[-1], near, local[1], *gates))
        weights.append(above)
        weights_away.append(away)
    far, gap = [], 1
    while gap < heights:
        lags = [n * gap for n in (1, 2, 3) if n * gap < heights]
        far += [(lag - 1, up(held, lag, False)) for lag in lags]
        for lag, (_, state) in zip(lags, far[-len(lags) :]):
            held = held + jnp.exp(-2.0 * span * lag * rates) * state
        gap *= 4
    wide = features // 2
    mine, theirs = lax.optimization_barrier((weights[last], weights_away[-1], local[-1]))[:2]
    finals = [swap(mine[:, :wide], TEAM), up(theirs[:, wide:], 1, True)]

    tables = [pltpu.VMEM((order, 8, LANES), f32)] * 2
    gated = [
        call(
            functools.partial(gate_kernel, part * some, [lag for lag, _ in far]),
            jax.ShapeDtypeStruct((some, TEAM * rows, LANES), bf16),
            tables + [pltpu.VMEM((rows // BLOCK, order, LANES), f32)],
            after=[local[-1]] if part < 2 else [weights[last], weights_away[-1]],
            micros=0.5,
        )(info, *gates, local[part], starts, rates, coef, near, *[state for _, state in far])
        for part in range(pieces)
    ]
    if not in_slots:
        gated = jnp.concatenate(gated, axis=0).transpose(1, 0, 2)
        gated = gated.reshape(TEAM * rows, width // (TEAM * depth), depth).transpose(1, 0, 2)
        gated = [gated]

    slots = [ref for pair in zip(weights, weights_away) for ref in pair] + [weights[last]]
    finished, joined = [], []
    for part, final in enumerate(finals):
        kept, sent = call(
            functools.partial(project_kernel, len(gated), in_slots, part * wide),
            [jax.ShapeDtypeStruct((2 * rows, wide), dtype) for dtype in (f32, bf16)],
            [pltpu.VMEM((TEAM * rows, wide), f32)],
            micros=1.0,
        )(group_info, *gated, *slots, final)
        mine_sum, away_sum = call(
            join_kernel,
            [jax.ShapeDtypeStruct((rows, wide), f32), jax.ShapeDtypeStruct((rows, wide), bf16)],
        )(info, kept, swap(sent, 1))
        joined.append(mine_sum)
        finished += [mine_sum, swap(away_sum, 2)]
    out = []
    for part in range(2):
        sums = finished[2 * part : 2 * part + 2]
        out = [finish(info, part * wide, features, *sums, out)]
    return out[0]


def solution(mesh):
    in_specs = (
        P(("groups", "seq"), None),
        P(("groups", "seq"), None),
        P(),
        P(),
        P(),
        P("seq", None),
    )
    out_specs = P(("groups", "seq"), None)
    return jax.shard_map(
        on_device, mesh=mesh, in_specs=in_specs, out_specs=out_specs, check_vma=False
    )
```

```python
import functools

import jax
import jax.numpy as jnp
from jax import lax
from jax.experimental import pallas as pl
from jax.experimental.pallas import tpu as pltpu
from jax.sharding import PartitionSpec as P

BLOCK = 32
LANES = 128
CHUNKS = 8
TEAM = 4
VMEM_LIMIT = 8 * 1024 * 1024

f32 = jnp.float32
bf16 = jnp.bfloat16


def tied(value, *others):
    return lax.optimization_barrier((value, *others))[0]


def call(kernel, out_shape, scratch=(), after=(), micros=0.0):
    def run(info, *args):
        return pl.pallas_call(
            kernel,
            out_shape=out_shape,
            in_specs=[pl.BlockSpec(memory_space=pltpu.SMEM)] + [pl.BlockSpec()] * len(args),
            scratch_shapes=list(scratch),
            compiler_params=pltpu.CompilerParams(vmem_limit_bytes=VMEM_LIMIT),
            cost_estimate=pl.CostEstimate(
                flops=int(micros * 1.1e9), bytes_accessed=int(micros * 3.6e6), transcendentals=0
            ),
        )(tied(info, *after), *args)

    return run


def deal_kernel(team, depth, plan, info_ref, *refs):
    me = info_ref[0]
    count = len(plan)
    sources, held, sems = refs[:count], refs[-1 - count : -1], refs[-1]
    outs = list(refs[count : -1 - count])
    copies = []
    for source, whole in zip(sources, held):
        wide = source.shape[1] // CHUNKS
        for chunk in range(CHUNKS):
            cols = slice(chunk * wide, (chunk + 1) * wide)
            sem = sems.at[len(copies)]
            copies.append(pltpu.make_async_copy(source.at[:, cols], whole.at[:, cols], sem))
            copies[-1].start()
    for source, whole, steps in zip(sources, held, plan):
        runs = source.shape[1] // (team * depth)
        mine = [outs.pop(0) for _ in range(steps)]
        for run in range(runs):
            if run % (runs // CHUNKS) == 0:
                copies.pop(0).wait()
            for step in range(steps):
                at = pl.multiple_of((run * team + (me ^ step)) * depth, depth)
                mine[step][:, run * depth : (run + 1) * depth] = whole[:, pl.ds(at, depth)]


def deal(info, team, depth, sources, plan):
    pieces = []
    if depth % LANES == 0:
        shapes = []
        for source, steps in zip(sources, plan):
            share = (source.shape[0], source.shape[1] // team)
            shapes += [jax.ShapeDtypeStruct(share, source.dtype)] * steps
        pieces = list(
            pl.pallas_call(
                functools.partial(deal_kernel, team, depth, plan),
                out_shape=shapes,
                in_specs=[pl.BlockSpec(memory_space=pltpu.SMEM)]
                + [pl.BlockSpec(memory_space=pltpu.HBM)] * len(sources),
                out_specs=[pl.BlockSpec(memory_space=pltpu.VMEM)] * len(shapes),
                scratch_shapes=[pltpu.VMEM(source.shape, source.dtype) for source in sources]
                + [pltpu.SemaphoreType.DMA((CHUNKS * len(sources),))],
                compiler_params=pltpu.CompilerParams(vmem_limit_bytes=VMEM_LIMIT),
            )(info, *sources)
        )
    else:
        for source, steps in zip(sources, plan):
            rows, width = source.shape
            cut = source.reshape(rows, width // (team * depth), team, depth)
            for step in range(steps):
                share = lax.dynamic_index_in_dim(cut, info[0] ^ step, 2, keepdims=False)
                pieces.append(share.reshape(rows, -1))
    return [[pieces.pop(0) for _ in range(steps)] for steps in plan]


def spread(values, me, lanes, wide, above):
    per = values[0].shape[0] // BLOCK
    for step in range(TEAM):
        for b in range(per):
            rows = values[step][b * BLOCK : (b + 1) * BLOCK, lanes].astype(f32)
            wide[(me ^ step) * per + b, above:, :] = rows


def tile_lanes(info_ref, slot):
    return pl.ds(pl.multiple_of(info_ref[3 + slot] * LANES, LANES), LANES)


def state_kernel(info_ref, *refs):
    values = refs[:TEAM]
    rate_ref, starts_ref, end_ref, wide = refs[TEAM:]
    order = rate_ref.shape[0]
    me = info_ref[0]

    @pl.loop(0, starts_ref.shape[0])
    def _(slot):
        lanes = tile_lanes(info_ref, slot)
        spread(values, me, lanes, wide, 0)
        rate = rate_ref[:, lanes]
        lam, lam8 = jnp.exp(-rate), jnp.exp(-8.0 * rate)

        def block(b, state):
            starts_ref[slot, b] = state
            for at in range(0, BLOCK, 8):
                inflow = jnp.broadcast_to(wide[b, at : at + 1, :], (order, LANES))
                for t in range(1, 8):
                    inflow = lam * inflow + wide[b, at + t : at + t + 1, :]
                state = lam8 * state + inflow
            return state

        zero = jnp.zeros((order, LANES), f32)
        end_ref[:, lanes] = lax.fori_loop(0, wide.shape[0], block, zero, unroll=4)


def taps_kernel(base, info_ref, *refs):
    values = refs[:TEAM]
    rate_ref, coef_ref, skip_ref, y_ref, wide, taps = refs[TEAM:]
    me = info_ref[0]
    wide[:, :BLOCK, :] = jnp.zeros((wide.shape[0], BLOCK, LANES), f32)

    @pl.loop(0, y_ref.shape[0])
    def _(slot):
        lanes = tile_lanes(info_ref, base + slot)
        spread(values, me, lanes, wide, BLOCK)
        skip = skip_ref[:, lanes]
        lam = jnp.exp(-rate_ref[:, lanes])
        power = coef_ref[:, lanes]
        for t in range(BLOCK):
            tap = jnp.sum(power, axis=0, keepdims=True).astype(bf16).astype(f32)
            taps[t] = jnp.broadcast_to(tap, (8, LANES))
            power = power * lam

        @pl.loop(0, wide.shape[0])
        def _(b):
            y = [skip * wide[b, BLOCK + 8 * i : BLOCK + 8 * i + 8, :] for i in range(BLOCK // 8)]
            for t in range(BLOCK):
                tap = taps[t]
                for i in range(t // 8, BLOCK // 8):
                    at = BLOCK + 8 * i - t
                    y[i] = y[i] + tap * wide[b, at : at + 8, :]
            for i in range(BLOCK // 8):
                y_ref[slot, pl.ds(pl.multiple_of(b * BLOCK + 8 * i, 8), 8), :] = y[i]


def pair_kernel(span, info_ref, end_ref, near_ref, rate_ref, out_ref):
    high = info_ref[1] == 1
    first = jnp.where(high, near_ref[...], end_ref[...])
    second = jnp.where(high, end_ref[...], near_ref[...])
    out_ref[...] = jnp.exp(-span * rate_ref[...]) * first + second


def gate_kernel(base, reaches, info_ref, *refs):
    gaps = len(reaches)
    gates = refs[:TEAM]
    y_ref, starts_ref, rate_ref, coef_ref, near_ref = refs[TEAM : TEAM + 5]
    far = refs[TEAM + 5 : TEAM + 5 + gaps]
    out_ref, reach, decay8, start = refs[TEAM + 5 + gaps :]
    me, high = info_ref[0], info_ref[1]
    order = rate_ref.shape[0]
    rows = gates[0].shape[0]
    per = rows // BLOCK
    span = float(TEAM * rows)
    ahead = lax.broadcasted_iota(jnp.int32, (8, LANES), 0).astype(f32) + 1.0

    @pl.loop(0, y_ref.shape[0])
    def _(slot):
        lanes = tile_lanes(info_ref, base + slot)
        rate, coef = rate_ref[:, lanes], coef_ref[:, lanes]
        for k in range(order):
            reach[k] = coef[k : k + 1] * jnp.exp(-ahead * rate[k : k + 1])
            decay8[k] = jnp.exp(jnp.broadcast_to(-8.0 * rate[k : k + 1], (8, LANES)))
        state = jnp.zeros((order, LANES), f32)
        for gap, ref in zip(reaches, far):
            state = state + jnp.exp(-2.0 * span * gap * rate) * ref[:, lanes]
        after = jnp.exp(-span * rate) * state + near_ref[:, lanes]
        state = jnp.where(high == 1, after, state)
        over = jnp.exp(-float(BLOCK) * rate)
        for step in range(TEAM):
            place = me ^ step
            goes = place ^ (me & 2)
            entering = state * jnp.exp(-(rows * place).astype(f32) * rate)
            for b in range(per):
                start[b] = starts_ref[base + slot, place * per + b] + entering
                entering = entering * over
            for b in range(per):
                y = []
                for i in range(BLOCK // 8):
                    here = pl.multiple_of(place * rows + b * BLOCK + 8 * i, 8)
                    y.append(y_ref[slot, pl.ds(here, 8), :])
                for k in range(order):
                    term = reach[k] * start[b, k : k + 1, :]
                    decay = decay8[k]
                    for i in range(BLOCK // 8):
                        y[i] = y[i] + term
                        if i + 1 < BLOCK // 8:
                            term = term * decay
                for i in range(0, BLOCK // 8, 2):
                    at = b * BLOCK + 8 * i
                    conv = jnp.concatenate(y[i : i + 2], axis=0)
                    gated = gates[step][at : at + 16, lanes].astype(f32) * conv
                    to = pl.ds(pl.multiple_of(goes * rows + at, 16), 16)
                    out_ref[slot, to, :] = gated.astype(bf16)


def product(pieces, in_slots, first, info_ref, gated, weights, into, before):
    per = gated[0].shape[0]
    wide = into.shape[1]
    step = min(wide, 512)
    slots = range(first, first + len(weights))
    if in_slots:
        left = [gated[slot // per][slot % per] for slot in slots]
    else:
        left = [gated[0][info_ref[3 + slot]] for slot in slots]
    left = jnp.concatenate(left, axis=1)
    for col in range(0, wide, step):
        cols = slice(col, col + step)
        right = jnp.concatenate([ref[:, cols] for ref in weights], axis=0)
        total = jnp.dot(left, right, preferred_element_type=f32)
        into[:, cols] = total if before is None else before[:, cols] + total


def project_kernel(pieces, in_slots, at, info_ref, *refs):
    gated, weights = refs[:pieces], refs[pieces:-3]
    kept_ref, sent_ref, total = refs[-3:]
    core = info_ref[2]
    rows, wide = kept_ref.shape[0] // 2, kept_ref.shape[1]
    weights = [ref.at[:, at : at + wide] for ref in weights[:-1]] + [weights[-1]]
    product(pieces, in_slots, 0, info_ref, gated, weights, total, None)
    for across in range(2):
        here = slice(across * rows, (across + 1) * rows)
        for which, out in enumerate((kept_ref, sent_ref)):
            start = (2 * across + (core ^ which)) * rows
            out[here, :] = total[pl.ds(pl.multiple_of(start, rows), rows), :].astype(out.dtype)


def join_kernel(info_ref, kept_ref, got_ref, mine_ref, away_ref):
    rows = mine_ref.shape[0]
    mine_ref[...] = kept_ref[:rows, :] + got_ref[:rows, :].astype(f32)
    away_ref[...] = (kept_ref[rows:, :] + got_ref[rows:, :].astype(f32)).astype(bf16)


def finish_kernel(at, info_ref, mine_ref, far_ref, *refs):
    out_ref, rounded, sem = refs[-3:]
    rounded[...] = (mine_ref[...] + far_ref[...].astype(f32)).astype(bf16)
    copy = pltpu.make_async_copy(rounded, out_ref.at[:, at : at + rounded.shape[1]], sem)
    copy.start()
    copy.wait()


def finish(info, at, features, mine, far, before):
    anywhere = pl.BlockSpec(memory_space=pl.ANY)
    return pl.pallas_call(
        functools.partial(finish_kernel, at),
        out_shape=jax.ShapeDtypeStruct((mine.shape[0], features), bf16),
        in_specs=[pl.BlockSpec(memory_space=pltpu.SMEM)]
        + [pl.BlockSpec()] * 2
        + [anywhere] * len(before),
        out_specs=anywhere,
        input_output_aliases={3: 0} if before else {},
        scratch_shapes=[pltpu.VMEM(mine.shape, bf16), pltpu.SemaphoreType.DMA],
        compiler_params=pltpu.CompilerParams(vmem_limit_bytes=VMEM_LIMIT),
    )(info, mine, far, *before)


def on_device(q_gate, values_in, decay_rate, residue, skip_gain, out_weight):
    rows, width = q_gate.shape
    depth, features = out_weight.shape
    order = decay_rate.shape[1]
    count = lax.axis_size("seq")
    heights = count // (2 * TEAM)
    mine = lax.axis_index("seq")
    me, core = mine % TEAM, mine % 2
    y, z = (mine // TEAM) % 2, mine // (2 * TEAM)
    share = width // TEAM

    def swap(value, bit):
        return lax.ppermute(value, "seq", [(i, i ^ bit) for i in range(count)])

    def up(value, gap, wrap):
        hop = gap * 2 * TEAM
        pairs = [(i, (i + hop) % count) for i in range(count) if wrap or i + hop < count]
        return lax.ppermute(value, "seq", pairs)

    in_slots = depth % LANES == 0
    groups = []
    for gap in range(heights):
        at = (z - gap) % heights
        groups += [at * 2 + y, at * 2 + (1 - y)]
    tiles = share // LANES
    order_of = groups if in_slots else list(range(tiles))
    info = jnp.stack([jnp.int32(n) for n in [me, y, core] + order_of])
    group_info = info if in_slots else jnp.stack([jnp.int32(n) for n in [me, y, core] + groups])

    def share_out(shares):
        return [shares[0]] + [swap(shares[step], step) for step in range(1, TEAM)]

    def next_round(block):
        return up(block, 1, True), swap(block, TEAM)

    last = heights - 1
    weights, weights_away = [out_weight], []
    if last > 0:
        above, away = next_round(out_weight)
        weights.append(above)
        weights_away.append(away)

    (values,) = deal(info, TEAM, depth, [values_in], [TEAM])
    values = share_out(values)
    gates, rates, residues, skip = deal(
        info, TEAM, depth, [q_gate, decay_rate.T, residue.T, skip_gain[None]], [TEAM, 1, 1, 1]
    )
    rates, residues, skip = rates[0], residues[0], skip[0]
    coef = residues * jnp.sqrt(-jnp.expm1(-2.0 * rates))
    gates = share_out(gates[:2] + [tied(gate, values[3]) for gate in gates[2:]])

    blocks = TEAM * rows // BLOCK
    starts, end = call(
        state_kernel,
        [
            jax.ShapeDtypeStruct((tiles, blocks, order, LANES), f32),
            jax.ShapeDtypeStruct((order, share), f32),
        ],
        [pltpu.VMEM((blocks, BLOCK, LANES), f32)],
        after=[weights[-1], weights_away[-1]],
        micros=0.5,
    )(info, *values, rates)

    pieces = 4
    some = tiles // pieces
    if len(weights) < heights:
        above, away = next_round(tied(weights[-1], weights_away[-1], rates, values[1]))
        weights.append(above)
        weights_away.append(away)
    local = []
    for part in range(pieces):
        local.append(
            call(
                functools.partial(taps_kernel, part * some),
                jax.ShapeDtypeStruct((some, TEAM * rows, LANES), f32),
                [pltpu.VMEM((blocks, 2 * BLOCK, LANES), f32), pltpu.VMEM((BLOCK, 8, LANES), f32)],
                after=[end] if part == 0 else [local[-1]] + ([weights[-1], weights_away[-1]] if part > 1 else []),
                micros=0.3,
            )(info, *values, rates, coef, skip)
        )

    near = swap(end, TEAM)
    end = tied(end, local[0], local[1], *gates)
    span = float(TEAM * rows)
    held = call(
        functools.partial(pair_kernel, span), jax.ShapeDtypeStruct((order, share), f32), micros=0.2
    )(info, end, near, rates)
    while len(weights) < heights:
        above, away = next_round(tied(weights[-1], weights_away[-1], near, local[1], *gates))
        weights.append(above)
        weights_away.append(away)
    far, gap = [], 1
    while gap < heights:
        lags = [n * gap for n in (1, 2, 3) if n * gap < heights]
        far += [(lag - 1, up(held, lag, False)) for lag in lags]
        for lag, (_, state) in zip(lags, far[-len(lags) :]):
            held = held + jnp.exp(-2.0 * span * lag * rates) * state
        gap *= 4
    wide = features // 2
    mine, theirs = lax.optimization_barrier((weights[last], weights_away[-1], local[-1]))[:2]
    finals = [swap(mine[:, :wide], TEAM), up(theirs[:, wide:], 1, True)]

    tables = [pltpu.VMEM((order, 8, LANES), f32)] * 2
    gated = [
        call(
            functools.partial(gate_kernel, part * some, [lag for lag, _ in far]),
            jax.ShapeDtypeStruct((some, TEAM * rows, LANES), bf16),
            tables + [pltpu.VMEM((rows // BLOCK, order, LANES), f32)],
            after=[local[-1]] if part < 2 else [weights[last], weights_away[-1]],
            micros=0.5,
        )(info, *gates, local[part], starts, rates, coef, near, *[state for _, state in far])
        for part in range(pieces)
    ]
    if not in_slots:
        gated = jnp.concatenate(gated, axis=0).transpose(1, 0, 2)
        gated = gated.reshape(TEAM * rows, width // (TEAM * depth), depth).transpose(1, 0, 2)
        gated = [gated]

    slots = [ref for pair in zip(weights, weights_away) for ref in pair] + [weights[last]]
    finished, joined = [], []
    for part, final in enumerate(finals):
        kept, sent = call(
            functools.partial(project_kernel, len(gated), in_slots, part * wide),
            [jax.ShapeDtypeStruct((2 * rows, wide), dtype) for dtype in (f32, bf16)],
            [pltpu.VMEM((TEAM * rows, wide), f32)],
            micros=1.0,
        )(group_info, *gated, *slots, final)
        mine_sum, away_sum = call(
            join_kernel,
            [jax.ShapeDtypeStruct((rows, wide), f32), jax.ShapeDtypeStruct((rows, wide), bf16)],
        )(info, kept, swap(sent, 1))
        joined.append(mine_sum)
        finished += [mine_sum, swap(away_sum, 2)]
    out = []
    for part in range(2):
        sums = finished[2 * part : 2 * part + 2]
        out = [finish(info, part * wide, features, *sums, out)]
    return out[0]


def solution(mesh):
    in_specs = (
        P(("groups", "seq"), None),
        P(("groups", "seq"), None),
        P(),
        P(),
        P(),
        P("seq", None),
    )
    out_specs = P(("groups", "seq"), None)
    return jax.shard_map(
        on_device, mesh=mesh, in_specs=in_specs, out_specs=out_specs, check_vma=False
    )
```
